32 devices in a mesh: dp: 4 (over x, core), fsdp: 8 (over z, y).
Axes of the slice: x: 2, y: 2, z: 4, core: 2. Of those that a mesh axis runs over, the one named last changes fastest.
Arguments:
- token_ids: int32 [32, 160], P(('dp', 'fsdp')), may hold values from 0 to 8191
- clip_ids: int32 [32, 160], P(('dp', 'fsdp')), may hold values from 0 to 2, never falling along the last dimension, each value on 1 to 80 neighbouring positions
- frame_ids: int32 [32, 160], P(('dp', 'fsdp')), may hold values from 0 to 7, never falling along the last dimension, each value on 1 to 40 neighbouring positions
- context_frames: int32 [32], P(('dp', 'fsdp')), may hold values from 0 to 3
- valid_mask: int32 [32, 160], P(('dp', 'fsdp')), may hold values from 0 to 1
- lookup_weight: float32 [8192, 2048], P(('dp', 'fsdp')), may hold values from -6 to 6
- lookup_moment: float32 [8192, 2048], P(('dp', 'fsdp')), may hold values from -4.8038765e-07 to 4.8038765e-07
- lookup_variance: float32 [8192, 2048], P(('dp', 'fsdp')), may hold values from 6.31763e-14 to 2.5032117e-13
- mixing_weight: float32 [2048, 6144], P(('dp', 'fsdp')), may hold values from -0.125 to 0.125
- mixing_moment: float32 [2048, 6144], P(('dp', 'fsdp')), may hold values from -4.8038765e-07 to 4.8038765e-07
- mixing_variance: float32 [2048, 6144], P(('dp', 'fsdp')), may hold values from 6.31763e-14 to 2.5032117e-13
- merging_weight: float32 [2048, 2048], P(('dp', 'fsdp')), may hold values from -0.5 to 0.5
- merging_moment: float32 [2048, 2048], P(('dp', 'fsdp')), may hold values from -4.8038765e-07 to 4.8038765e-07
- merging_variance: float32 [2048, 2048], P(('dp', 'fsdp')), may hold values from 6.31763e-14 to 2.5032117e-13
- widening_weight: float32 [2048, 8192], P(('dp', 'fsdp')), may hold values from -0.125 to 0.125
- widening_moment: float32 [2048, 8192], P(('dp', 'fsdp')), may hold values from -4.8038765e-07 to 4.8038765e-07
- widening_variance: float32 [2048, 8192], P(('dp', 'fsdp')), may hold values from 6.31763e-14 to 2.5032117e-13
- narrowing_weight: float32 [8192, 2048], P(('dp', 'fsdp')), may hold values from -0.0625 to 0.0625
- narrowing_moment: float32 [8192, 2048], P(('dp', 'fsdp')), may hold values from -4.8038765e-07 to 4.8038765e-07
- narrowing_variance: float32 [8192, 2048], P(('dp', 'fsdp')), may hold values from 6.31763e-14 to 2.5032117e-13
- readout_weight: float32 [2048, 8192], P(('dp', 'fsdp')), may hold values from -0.1875 to 0.1875
- readout_moment: float32 [2048, 8192], P(('dp', 'fsdp')), may hold values from -4.8038765e-07 to 4.8038765e-07
- readout_variance: float32 [2048, 8192], P(('dp', 'fsdp')), may hold values from 6.31763e-14 to 2.5032117e-13
- scaling_weight: float32 [3, 2048], P(None, ('dp', 'fsdp')), may hold values from 0.2 to 2.2, as said below
- scaling_moment: float32 [3, 2048], P(None, ('dp', 'fsdp')), may hold values from -4.8038764e-06 to 4.8038764e-06
- scaling_variance: float32 [3, 2048], P(None, ('dp', 'fsdp')), may hold values from 6.3176296e-12 to 2.5032117e-11
Outputs:
- loss_terms: float32 [4], replicated
- grad_norm: float32 [], replicated
- lookup_master: float32 [8192, 2048], P(('dp', 'fsdp'))
- lookup_mean: float32 [8192, 2048], P(('dp', 'fsdp'))
- lookup_square: float32 [8192, 2048], P(('dp', 'fsdp'))
- lookup_copy: bfloat16 [8192, 2048], P(('dp', 'fsdp'))
- mixing_master: float32 [2048, 6144], P(('dp', 'fsdp'))
- mixing_mean: float32 [2048, 6144], P(('dp', 'fsdp'))
- mixing_square: float32 [2048, 6144], P(('dp', 'fsdp'))
- mixing_copy: bfloat16 [2048, 6144], P(('dp', 'fsdp'))
- merging_master: float32 [2048, 2048], P(('dp', 'fsdp'))
- merging_mean: float32 [2048, 2048], P(('dp', 'fsdp'))
- merging_square: float32 [2048, 2048], P(('dp', 'fsdp'))
- merging_copy: bfloat16 [2048, 2048], P(('dp', 'fsdp'))
- widening_master: float32 [2048, 8192], P(('dp', 'fsdp'))
- widening_mean: float32 [2048, 8192], P(('dp', 'fsdp'))
- widening_square: float32 [2048, 8192], P(('dp', 'fsdp'))
- widening_copy: bfloat16 [2048, 8192], P(('dp', 'fsdp'))
- narrowing_master: float32 [8192, 2048], P(('dp', 'fsdp'))
- narrowing_mean: float32 [8192, 2048], P(('dp', 'fsdp'))
- narrowing_square: float32 [8192, 2048], P(('dp', 'fsdp'))
- narrowing_copy: bfloat16 [8192, 2048], P(('dp', 'fsdp'))
- readout_master: float32 [2048, 8192], P(('dp', 'fsdp'))
- readout_mean: float32 [2048, 8192], P(('dp', 'fsdp'))
- readout_square: float32 [2048, 8192], P(('dp', 'fsdp'))
- readout_copy: bfloat16 [2048, 8192], P(('dp', 'fsdp'))
- scaling_master: float32 [3, 2048], P(None, ('dp', 'fsdp'))
- scaling_mean: float32 [3, 2048], P(None, ('dp', 'fsdp'))
- scaling_square: float32 [3, 2048], P(None, ('dp', 'fsdp'))
The draws below stay inside these ranges and needn't reach their ends.
Inputs may be any that keep to these rules, and one draw needn't show every extreme that they name: `scaling_weight`: positive.
All inputs are finite; a program needn't handle non-finite values.
Results may differ from the reference program's by a relative error of at most 0.006.
The reference program's roundings to bfloat16 on the way count: a program that leaves them out, or rounds other values in their place, can miss the bound.
Values may be sent and summed in bfloat16 or wider, within the bound.
No kernel may reach another device: no remote copies, remote signals or barrier semaphores. Data moves between devices by JAX's collectives and lax.ppermute only.
A program may use at most 528 MiB of HBM per device.

```python
import math
import jax
import jax.numpy as jnp
import numpy as np
from jax import lax

D = 2048
HEADS = 16
FF = 8192
V = 8192
LEN = 160
FRAMES = 8
STEP = 5
BATCH = 32
SEQS_GROUP = 8
PARAMS = 83892224


def draw_valid_mask(key, part):
    key = jax.random.fold_in(key, 11)
    row_index = jnp.arange(BATCH, dtype=jnp.int32)
    outer_index = row_index // SEQS_GROUP
    inner_index = row_index % SEQS_GROUP
    outer_span = max(BATCH // SEQS_GROUP - 1, 1)
    inner_span = max(SEQS_GROUP - 1, 1)
    percent = 12 + 38 * outer_index // outer_span + 45 * inner_index // inner_span
    rolled = jax.random.randint(key, (BATCH, LEN), 0, 100)
    return (rolled < percent[:, None]).astype(jnp.int32)


def draw_scaling_weight(key, part):
    key = jax.random.fold_in(key, 13)
    ramp = jnp.arange(D, dtype=jnp.float32) / (D - 1)
    base = 0.5 + ramp
    noise = jax.random.uniform(key, (3, D), jnp.float32, 0.8, 1.2)
    return (base[None, :] * noise).astype(jnp.float32)


def plant(array, rng, least, top_value):
    extent = array.shape
    place = [jax.random.randint(jax.random.fold_in(rng, axis), (), 0, extent[axis]) for axis in range(len(extent))]
    array = array.at[tuple(place)].set(least)
    longest = extent.index(max(extent))
    place[longest] = (place[longest] + 1) % extent[longest]
    return array.at[tuple(place)].set(top_value)


def steps_of(stream_key, dims, shards, smallest, largest):
    level = 1.0
    for dim, shards_of in shards:
        draws = jax.random.uniform(jax.random.fold_in(jax.random.fold_in(stream_key, 6), dim), (shards_of,), jnp.float32, smallest / len(shards), largest / len(shards))
        level = level * jnp.repeat(jnp.exp(draws), dims[dim] // shards_of).reshape((-1,) + (1,) * (len(dims) - 1 - dim))
    return level


def cumulative_ranks(number_of, lean):
    portions = [(1 << 20) // math.isqrt(grade ** lean) + 1 for grade in range(1, number_of + 1)]
    deviation = 1 + sum(portions) // (1 << 30)
    return np.cumsum(np.array([max(1, weight // deviation) for weight in portions]))


def skewed_ids(rng, shape, count, slope):
    table = cumulative_ranks(count, slope)
    ticket = jax.random.randint(jax.random.fold_in(rng, 1), shape, 0, int(table[count - 1]))
    grade = jnp.searchsorted(jnp.asarray(table, jnp.int32), ticket, side="right")
    return jax.random.permutation(jax.random.fold_in(rng, 2), count)[grade].astype(jnp.int32)


def length_profile(count, total, bound, skew):
    weights = [(1 << 20) // math.isqrt(grade ** skew) + 1 for grade in range(2, count + 1)]
    rest, counts = total - bound - (count - 1), [1] * (count - 1)
    while rest > 0:
        movable = [i for i in range(count - 1) if counts[i] < bound]
        whole, left = sum([weights[i] for i in movable]), rest
        for i in movable:
            extra = min(bound - counts[i], max(1, left * weights[i] // whole), rest)
            counts[i] = counts[i] + extra
            rest = rest - extra
    return np.array([bound] + counts)


def ragged_sizes(stream_key, number_of, total, reach, lean):
    if number_of == 2:
        one = jax.random.randint(stream_key, (), max(1, total - reach), min(reach, total - 1) + 1)
        return jnp.stack([one, total - one])
    lengths = jnp.asarray(length_profile(number_of, total, reach, lean), jnp.int32)
    couples = (number_of - 1) // 2
    source_of, taker = lengths[1:1 + 2 * couples:2], lengths[2:2 + 2 * couples:2]
    margin = jnp.minimum(source_of - 1, reach - taker)
    shifted = jax.random.randint(jax.random.fold_in(stream_key, 1), (couples,), 0, 1 << 20) % (margin + 1)
    lengths = lengths.at[1:1 + 2 * couples:2].set(source_of - shifted).at[2:2 + 2 * couples:2].set(taker + shifted)
    return lengths[jax.random.permutation(jax.random.fold_in(stream_key, 2), number_of)]


def gaussian(own_key, dims, width, bound, shards=(), held_as=jnp.bfloat16):
    loudness = steps_of(own_key, dims, shards, -0.22, 0.18) if shards else 1.0
    array = jax.random.normal(own_key, dims, jnp.float32) * width * loudness
    return jnp.minimum(jnp.maximum(array, -bound), bound).astype(held_as)


def setup_inputs(seed: int = 0) -> dict:
    key_of = jax.random.split(jax.random.key(seed), 27)
    token_ids = plant(skewed_ids(key_of[0], (BATCH, LEN), V, 2), jax.random.fold_in(key_of[0], 3), 0, V - 1).astype(jnp.int32)
    clip_ids = jax.vmap(lambda own: jnp.searchsorted(jnp.cumsum(ragged_sizes(own, 3, LEN, LEN // 2, 2)), jnp.arange(LEN), side="right"))(jax.random.split(key_of[1], BATCH)).reshape((BATCH, LEN)).astype(jnp.int32)
    frame_ids = jax.vmap(lambda own: jnp.searchsorted(jnp.cumsum(ragged_sizes(own, FRAMES, LEN, LEN // 4, 2)), jnp.arange(LEN), side="right"))(jax.random.split(key_of[2], BATCH)).reshape((BATCH, LEN)).astype(jnp.int32)
    context_frames = plant(jax.random.randint(key_of[3], (BATCH,), 0, FRAMES // 2), jax.random.fold_in(key_of[3], 1), 0, (FRAMES // 2) - 1).astype(jnp.int32)
    valid_mask = draw_valid_mask(jax.random.fold_in(key_of[26], 71), 0)
    lookup_weight = gaussian(key_of[5], (V, D), 1.0, 6.0, ((0, 32),), jnp.float32)
    lookup_moment = gaussian(key_of[6], (V, D), (0.00111 / PARAMS ** 0.5), 4.803876549885899e-07, ((0, 32),), jnp.float32)
    lookup_variance = jnp.clip(jnp.exp(math.log(2.503211667895938e-13) - 1.3768156 * jax.random.uniform(key_of[7], (V, D), jnp.float32) ** steps_of(key_of[7], (V, D), ((0, 32),), -0.2, 0.2)), 6.317629796040447e-14, 2.503211667895938e-13)
    mixing_weight = gaussian(key_of[8], (D, 3 * D), D ** -0.5, 0.125, ((0, 32),), jnp.float32)
    mixing_moment = gaussian(key_of[9], (D, 3 * D), (0.00111 / PARAMS ** 0.5), 4.803876549885899e-07, ((0, 32),), jnp.float32)
    mixing_variance = jnp.clip(jnp.exp(math.log(2.503211667895938e-13) - 1.3768156 * jax.random.uniform(key_of[10], (D, 3 * D), jnp.float32) ** steps_of(key_of[10], (D, 3 * D), ((0, 32),), -0.2, 0.2)), 6.317629796040447e-14, 2.503211667895938e-13)
    merging_weight = gaussian(key_of[11], (D, D), (D // 16) ** -0.5, 0.5, ((0, 32),), jnp.float32)
    merging_moment = gaussian(key_of[12], (D, D), (0.00111 / PARAMS ** 0.5), 4.803876549885899e-07, ((0, 32),), jnp.float32)
    merging_variance = jnp.clip(jnp.exp(math.log(2.503211667895938e-13) - 1.3768156 * jax.random.uniform(key_of[13], (D, D), jnp.float32) ** steps_of(key_of[13], (D, D), ((0, 32),), -0.2, 0.2)), 6.317629796040447e-14, 2.503211667895938e-13)
    widening_weight = gaussian(key_of[14], (D, FF), D ** -0.5, 0.125, ((0, 32),), jnp.float32)
    widening_moment = gaussian(key_of[15], (D, FF), (0.00111 / PARAMS ** 0.5), 4.803876549885899e-07, ((0, 32),), jnp.float32)
    widening_variance = jnp.clip(jnp.exp(math.log(2.503211667895938e-13) - 1.3768156 * jax.random.uniform(key_of[16], (D, FF), jnp.float32) ** steps_of(key_of[16], (D, FF), ((0, 32),), -0.2, 0.2)), 6.317629796040447e-14, 2.503211667895938e-13)
    narrowing_weight = gaussian(key_of[17], (FF, D), FF ** -0.5, 0.0625, ((0, 32),), jnp.float32)
    narrowing_moment = gaussian(key_of[18], (FF, D), (0.00111 / PARAMS ** 0.5), 4.803876549885899e-07, ((0, 32),), jnp.float32)
    narrowing_variance = jnp.clip(jnp.exp(math.log(2.503211667895938e-13) - 1.3768156 * jax.random.uniform(key_of[19], (FF, D), jnp.float32) ** steps_of(key_of[19], (FF, D), ((0, 32),), -0.2, 0.2)), 6.317629796040447e-14, 2.503211667895938e-13)
    readout_weight = gaussian(key_of[20], (D, V), (D // 2) ** -0.5, 0.1875, ((0, 32),), jnp.float32)
    readout_moment = gaussian(key_of[21], (D, V), (0.00111 / PARAMS ** 0.5), 4.803876549885899e-07, ((0, 32),), jnp.float32)
    readout_variance = jnp.clip(jnp.exp(math.log(2.503211667895938e-13) - 1.3768156 * jax.random.uniform(key_of[22], (D, V), jnp.float32) ** steps_of(key_of[22], (D, V), ((0, 32),), -0.2, 0.2)), 6.317629796040447e-14, 2.503211667895938e-13)
    scaling_weight = draw_scaling_weight(jax.random.fold_in(key_of[26], 71), 0)
    scaling_moment = gaussian(key_of[24], (3, D), (0.0111 / PARAMS ** 0.5), 4.8038764361990616e-06, ((1, 32),), jnp.float32)
    scaling_variance = jnp.clip(jnp.exp(math.log(2.5032117004220034e-11) - 1.3768156 * jax.random.uniform(key_of[25], (3, D), jnp.float32) ** steps_of(key_of[25], (3, D), ((1, 32),), -0.2, 0.2)), 6.3176295792000126e-12, 2.5032117004220034e-11)
    return {"token_ids": token_ids, "clip_ids": clip_ids, "frame_ids": frame_ids, "context_frames": context_frames, "valid_mask": valid_mask, "lookup_weight": lookup_weight, "lookup_moment": lookup_moment, "lookup_variance": lookup_variance, "mixing_weight": mixing_weight, "mixing_moment": mixing_moment, "mixing_variance": mixing_variance, "merging_weight": merging_weight, "merging_moment": merging_moment, "merging_variance": merging_variance, "widening_weight": widening_weight, "widening_moment": widening_moment, "widening_variance": widening_variance, "narrowing_weight": narrowing_weight, "narrowing_moment": narrowing_moment, "narrowing_variance": narrowing_variance, "readout_weight": readout_weight, "readout_moment": readout_moment, "readout_variance": readout_variance, "scaling_weight": scaling_weight, "scaling_moment": scaling_moment, "scaling_variance": scaling_variance}


@jax.custom_vjp
def low(v):
    return lax.optimization_barrier(v.astype(jnp.bfloat16)).astype(jnp.float32)

@jax.custom_vjp
def low_back(v):
    return v

def low_keep(v):
    return (low(v), None)

def low_pass(kept, grad):
    return (grad,)

def back_keep(v):
    return (v, None)

def back_low(kept, grad):
    return (low(grad),)
low.defvjp(low_keep, low_pass)
low_back.defvjp(back_keep, back_low)
BETA_FIRST = 0.9
BETA_SECOND = 0.95
ADAM_EPSILON = 1e-08
SQUARE_COEF = 0.01
CLIP_NORM = 0.01
NORM_EPSILON = 1e-05
LEARN_RATES = (0.5, 0.02, 0.02, 0.02, 0.012, 0.02, 0.3)
DECAY_RATES = (0.1, 0.1, 0.1, 0.1, 0.1, 0.1, 0.0)
PRECISE = lax.Precision.HIGHEST

def rms_scale(values, gain_row):
    return values * lax.rsqrt(lax.optimization_barrier(jnp.mean(values * values, axis=-1, keepdims=True)) + NORM_EPSILON) * gain_row

def matmul(left_side, right_side):
    return jnp.dot(left_side, right_side, precision=PRECISE, preferred_element_type=jnp.float32)

def target_masks(token_ids, clip_ids, frame_ids, context_frames, valid_mask):
    next_ids = jnp.concatenate([token_ids[:, 1:], jnp.zeros_like(token_ids[:, :1])], axis=1)
    never = jnp.zeros_like(clip_ids[:, :1]) > 0
    same_clip = jnp.concatenate([clip_ids[:, 1:] == clip_ids[:, :-1], never], axis=1)
    after_context = jnp.concatenate([frame_ids[:, 1:] > context_frames[:, None], never], axis=1)
    counted = ((valid_mask > 0) & same_clip & after_context).astype(jnp.float32)
    return (next_ids, counted, valid_mask.astype(jnp.float32))

def block_sums(weights, token_ids, clip_ids, frame_ids, next_ids, counted, valid):
    lookup, mixing, merging, widening, narrowing, readout, gain_rows = weights
    seq_count, length = token_ids.shape
    token_count = seq_count * length
    model_width = mixing.shape[0]
    head_size = model_width // HEADS
    embedded = lookup[token_ids.reshape(-1)]
    normed_one = low(rms_scale(embedded, gain_rows[0]))
    joint = low(low_back(matmul(normed_one, mixing)))
    query_heads = joint[:, :model_width].reshape(seq_count, length, HEADS, head_size)
    key_heads = joint[:, model_width:2 * model_width].reshape(seq_count, length, HEADS, head_size)
    value_heads = joint[:, 2 * model_width:].reshape(seq_count, length, HEADS, head_size)
    scores = low_back(jnp.einsum('bqhd,bkhd->bhqk', query_heads, key_heads, precision=PRECISE) * head_size ** (-0.5))
    allowed = (clip_ids[:, :, None] == clip_ids[:, None, :]) & (frame_ids[:, None, :] <= frame_ids[:, :, None])
    scores = jnp.where(allowed[:, None], scores, -1e+30)
    attend = low(jax.nn.softmax(scores, axis=-1))
    mixed_heads = low(low_back(jnp.einsum('bhqk,bkhd->bqhd', attend, value_heads, precision=PRECISE).reshape(token_count, model_width)))
    stream_one = embedded + low_back(matmul(mixed_heads, merging))
    normed_two = low(rms_scale(stream_one, gain_rows[1]))
    widened = low_back(matmul(normed_two, widening))
    stream_two = stream_one + low_back(matmul(low(jax.nn.gelu(widened)), narrowing))
    normed_three = low(rms_scale(stream_two, gain_rows[2]))
    logits = low_back(matmul(normed_three, readout))
    log_total = jax.nn.logsumexp(logits, axis=-1)
    picked = jnp.take_along_axis(logits, next_ids.reshape(-1, 1), axis=1)[:, 0]
    cross_sum = jnp.sum((log_total - picked) * counted.reshape(-1))
    square_sum = jnp.sum(log_total * log_total * valid.reshape(-1))
    return jnp.stack([cross_sum, square_sum])

def adam_update(master, moment, variance, gradient, rate, decay):
    new_mean = BETA_FIRST * moment + (1.0 - BETA_FIRST) * gradient
    new_square = BETA_SECOND * variance + (1.0 - BETA_SECOND) * gradient * gradient
    mean_hat = new_mean / (1.0 - BETA_FIRST ** STEP)
    square_hat = new_square / (1.0 - BETA_SECOND ** STEP)
    new_master = master - rate * (mean_hat / (jnp.sqrt(square_hat) + ADAM_EPSILON) + decay * master)
    return (new_master, new_mean, new_square)

def reference(token_ids, clip_ids, frame_ids, context_frames, valid_mask, lookup_weight, lookup_moment, lookup_variance, mixing_weight, mixing_moment, mixing_variance, merging_weight, merging_moment, merging_variance, widening_weight, widening_moment, widening_variance, narrowing_weight, narrowing_moment, narrowing_variance, readout_weight, readout_moment, readout_variance, scaling_weight, scaling_moment, scaling_variance):
    next_ids, counted, valid = target_masks(token_ids, clip_ids, frame_ids, context_frames, valid_mask)
    mask_count = jnp.sum(counted)
    valid_count = jnp.sum(valid)
    masters = (lookup_weight, mixing_weight, merging_weight, widening_weight, narrowing_weight, readout_weight, scaling_weight)
    moments = (lookup_moment, mixing_moment, merging_moment, widening_moment, narrowing_moment, readout_moment, scaling_moment)
    variances = (lookup_variance, mixing_variance, merging_variance, widening_variance, narrowing_variance, readout_variance, scaling_variance)
    block_seqs = 16 if BATCH % 16 == 0 else BATCH
    shaped = tuple((source.reshape((BATCH // block_seqs, block_seqs) + source.shape[1:]) for source in (token_ids, clip_ids, frame_ids, next_ids, counted, valid)))
    summed = jax.checkpoint(block_sums)

    def loss_of(params):
        weights = tuple((low(master) for master in params))

        def one_block(running, pieces):
            return (running + summed(weights, *pieces), None)
        loss_sums, _ = lax.scan(one_block, jnp.zeros((2,), jnp.float32), shaped)
        return (loss_sums[0] / mask_count + SQUARE_COEF * loss_sums[1] / valid_count, loss_sums)
    loss_value, pullback, loss_sums = jax.vjp(loss_of, masters, has_aux=True)
    gradients = pullback(jnp.ones_like(loss_value))[0]
    norm_value = jnp.sqrt(sum((jnp.sum(gradient * gradient) for gradient in gradients)))
    clip_factor = jnp.minimum(1.0, CLIP_NORM / norm_value)
    updated = [adam_update(masters[index], moments[index], variances[index], gradients[index] * clip_factor, LEARN_RATES[index], DECAY_RATES[index]) for index in range(7)]
    loss_terms = jnp.stack([loss_sums[0], mask_count, loss_sums[1], valid_count])
    bf16 = jnp.bfloat16
    return (loss_terms, norm_value, updated[0][0], updated[0][1], updated[0][2], updated[0][0].astype(bf16), updated[1][0], updated[1][1], updated[1][2], updated[1][0].astype(bf16), updated[2][0], updated[2][1], updated[2][2], updated[2][0].astype(bf16), updated[3][0], updated[3][1], updated[3][2], updated[3][0].astype(bf16), updated[4][0], updated[4][1], updated[4][2], updated[4][0].astype(bf16), updated[5][0], updated[5][1], updated[5][2], updated[5][0].astype(bf16), updated[6][0], updated[6][1], updated[6][2])
```

```python
import functools

import jax
import jax.numpy as jnp
from jax import lax
from jax.experimental import pallas as pl
from jax.experimental.pallas import tpu as pltpu
from jax.sharding import Mesh
from jax.sharding import PartitionSpec as P

HEADS = 16
STEP = 5

BETA_FIRST = 0.9
BETA_SECOND = 0.95
ADAM_EPSILON = 1e-08
SQUARE_COEF = 0.01
CLIP_NORM = 0.01
NORM_EPSILON = 1e-05
LEARN_RATES = (0.5, 0.02, 0.02, 0.02, 0.012, 0.02, 0.3)
DECAY_RATES = (0.1, 0.1, 0.1, 0.1, 0.1, 0.1, 0.0)

ALL = ("u", "c", "a", "t", "b")
GROUP = ("u", "c", "t")
HALF = jnp.bfloat16
FULL = jnp.float32
WIRE_HALF = (HALF, HALF, HALF)
WIRE_FORWARD = (HALF, HALF, HALF)
WIRE_BACK = (HALF, HALF, HALF)
SLICE_WIRE = FULL


class Layout:
    def __init__(self, mesh):
        dp, fsdp = mesh.shape["dp"], mesh.shape["fsdp"]
        self.devices = dp * fsdp
        self.b = self.devices // HEADS
        self.a = fsdp // (2 * self.b)
        self.u = dp // 2
        self.mesh = Mesh(mesh.devices.reshape(self.u, 2, self.a, 2, self.b), ALL)
        self.sizes = {"u": self.u, "c": 2, "a": self.a, "t": 2, "b": self.b}

    def swap(self, value, axis, bit=1):
        return lax.ppermute(value, axis, [(i, i ^ bit) for i in range(self.sizes[axis])])

    def swap_group(self, value, ju, jc, jt):
        mask = ju * 4 + jc * 2 + jt
        return lax.ppermute(value, GROUP, [(i, i ^ mask) for i in range(4 * self.u)])

    def swap_first(self, value):
        return lax.ppermute(value, GROUP, [(i, i ^ (1 if i & 2 else 4)) for i in range(4 * self.u)])

    def swap_second(self, value):
        return lax.ppermute(value, GROUP, [(i, i ^ (4 if i & 2 else 1)) for i in range(4 * self.u)])

    def bits(self, axis):
        return [1 << k for k in range(self.sizes[axis].bit_length() - 1)]


def to_full(value):
    return value.astype(FULL)


def after(value, others):
    return value if others is None else lax.optimization_barrier((value, others))[0]


def gather_group(lay, block, middle=None, end=None):
    first, second = after(lay.swap_first(block), middle), lay.swap_second(block)
    near = [block, first, second, lay.swap_second(first)]
    blocks = near + [lay.swap(part, "c") for part in near]
    blocks[-1] = after(blocks[-1], end)
    rows = block.shape[0]

    def plan(index):
        return [(i, None, 0, (pl.ds(i * rows, rows),)) for i in range(8)]

    return move(plan, [(8 * rows, block.shape[1])], blocks)[0]


def scatter_group(lay, near, far, wire, middle=None, end=None):
    rows = near.shape[0] // 4
    half = to_full(near) + to_full(lay.swap(far.astype(wire[0]), "c"))
    second = after(lay.swap_second(half[2 * rows :].astype(wire[1])), middle)
    pair = half[: 2 * rows] + to_full(second)
    first = after(lay.swap_first(pair[rows:].astype(wire[2])), end)
    return pair[:rows] + to_full(first)


class Copies:
    def __init__(self, lay, piece, token):
        piece = after(piece, token)
        self.lay, self.pieces = lay, {(0, 0): piece}
        for bit in lay.bits("a"):
            for key in list(self.pieces):
                self.pieces[key[0] | bit, key[1]] = lay.swap(self.pieces[key], "a", bit)
        self.over_a = [piece for key, piece in self.pieces.items() if key != (0, 0)]

    def finish(self):
        for bit in self.lay.bits("b"):
            for key in list(self.pieces):
                self.pieces[key[0], key[1] | bit] = self.lay.swap(self.pieces[key], "b", bit)
        return self.pieces


class Reduction:
    def __init__(self, lay, pieces):
        self.lay, self.pieces = lay, dict(pieces)
        self.steps = [(axis, bit) for axis in ("b", "a") for bit in reversed(lay.bits(axis))]

    def prepare(self):
        axis, bit = self.steps[0]
        spot = 0 if axis == "a" else 1
        keys = [key for key in self.pieces if key[spot] & bit]
        self.sent = {key: self.pieces.pop(key).astype(HALF) for key in keys}
        return list(self.sent.values())

    def step(self, start=None, end=None):
        axis, bit = self.steps.pop(0)
        came_in = []
        for key, sent in self.sent.items():
            kept = (key[0] ^ bit, key[1]) if axis == "a" else (key[0], key[1] ^ bit)
            came = after(self.lay.swap(after(sent, start), axis, bit), end)
            self.pieces[kept] = to_full(self.pieces[kept]) + to_full(came)
            came_in.append(came)
        return came_in

    def finish(self):
        while self.steps:
            self.prepare()
            self.step()
        return self.pieces[0, 0]


def move_kernel(plan, sources, targets, *refs):
    index = {axis: lax.axis_index(axis) for axis in ALL}
    ins, outs, sems = refs[:sources], refs[sources : sources + targets], refs[sources + targets]
    copies = []
    for number, (source, at_source, target, at_target) in enumerate(plan(index)):
        from_ref = ins[source] if at_source is None else ins[source].at[at_source]
        to_ref = outs[target] if at_target is None else outs[target].at[at_target]
        copies.append(pltpu.make_async_copy(from_ref, to_ref, sems.at[number]))
    for copy in copies:
        copy.start()
    for copy in copies:
        copy.wait()


def move(plan, shapes, sources):
    count = len(plan({axis: 0 for axis in ALL}))
    kind = sources[0].dtype
    return pl.pallas_call(
        functools.partial(move_kernel, plan, len(sources), len(shapes)),
        out_shape=[jax.ShapeDtypeStruct(shape, kind) for shape in shapes],
        in_specs=[pl.BlockSpec(memory_space=pl.ANY)] * len(sources),
        out_specs=[pl.BlockSpec(memory_space=pltpu.VMEM)] * len(shapes),
        scratch_shapes=[pltpu.SemaphoreType.DMA((count,))],
        compiler_params=pltpu.CompilerParams(vmem_limit_bytes=16 * 2**20),
        cost_estimate=pl.CostEstimate(
            flops=0,
            bytes_accessed=2 * sum(s.size * s.dtype.itemsize for s in sources),
            transcendentals=0,
        ),
    )(*sources)


GROUP_OFFSETS = [(ju, jc, jt) for ju in (0, 1) for jc in (0, 1) for jt in (0, 1)]


def member(index, offsets):
    return tuple(index[axis] ^ offset for axis, offset in zip(GROUP, offsets))


def swap_members(lay, blocks):
    return list(blocks[:1]) + [
        lay.swap_group(block, *offsets) for block, offsets in zip(blocks[1:], GROUP_OFFSETS[1:])
    ]


def gather_rows(lay, parts):
    pieces = [part.finish() for part in parts]
    rows, width = pieces[0][0, 0].shape
    sources = [(part, key) for part in range(len(parts)) for key in pieces[part]]

    def plan(index):
        return [
            (i, None, 0, (index["a"] ^ ja, index["b"] ^ jb, part))
            for i, (part, (ja, jb)) in enumerate(sources)
        ]

    shape = (lay.a, lay.b, len(parts), rows, width)
    full = move(plan, [shape], [pieces[part][key] for part, key in sources])[0]
    return full.reshape(-1, width)


def spread_slices(lay, shards, spans, start):
    rows = shards[0].shape[0]
    widths = [sum(size for _, size in span(0, 0, 0)) for span in spans]

    def pick(index):
        copies = []
        for i, offsets in enumerate(GROUP_OFFSETS):
            done = 0
            for number, span in enumerate(spans):
                for start, size in span(*member(index, offsets)):
                    copies.append(
                        (number, (slice(None), pl.ds(start, size)), i, (slice(None), pl.ds(done, size)))
                    )
                    done += size
        return copies

    def pile(index):
        copies = []
        for i in range(8):
            done = 0
            for number, width in enumerate(widths):
                copies.append((i, (slice(None), pl.ds(done, width)), number, (i,)))
                done += width
        return copies

    blocks = [after(block, start) for block in move(pick, [(rows, sum(widths))] * 8, shards)]
    received = swap_members(lay, blocks)
    return move(pile, [(8, rows, width) for width in widths], received)


def gather_slices(lay, copies):
    pieces = copies.finish()
    _, rows, width = pieces[0, 0].shape
    keys = list(pieces)

    def plan(index):
        moves = []
        for i, (ja, jb) in enumerate(keys):
            for slot, offsets in enumerate(GROUP_OFFSETS):
                u, c, t = member(index, offsets)
                moves.append((i, (slot,), 0, (u, c, index["a"] ^ ja, t, index["b"] ^ jb)))
        return moves

    shape = (lay.u, 2, lay.a, 2, lay.b, rows, width)
    return move(plan, [shape], [pieces[key] for key in keys])[0].reshape(-1, width)


def reduce_rows(lay, gradient):
    me_a, me_b = lax.axis_index("a"), lax.axis_index("b")
    shaped = gradient.reshape(lay.a, lay.b, -1, gradient.shape[1])
    return Reduction(
        lay,
        {
            (ja, jb): lax.dynamic_slice(
                shaped, (me_a ^ ja, me_b ^ jb, 0, 0), (1, 1) + shaped.shape[2:]
            )[0, 0]
            for ja in range(lay.a)
            for jb in range(lay.b)
        },
    )


def reduce_slices(lay, gradient):
    me_a, me_b = lax.axis_index("a"), lax.axis_index("b")
    width = gradient.shape[1]
    shaped = gradient.reshape(lay.u * 2, lay.a, 2, lay.b, -1, width)
    size = (lay.u * 2, 1, 2, 1, shaped.shape[4], width)
    return Reduction(
        lay,
        {
            (ja, jb): lax.dynamic_slice(shaped, (0, me_a ^ ja, 0, me_b ^ jb, 0, 0), size)[:, 0, :, 0]
            for ja in range(lay.a)
            for jb in range(lay.b)
        },
    )


def member_blocks(lay, summed):
    shaped = summed.reshape((lay.u, 2, 2) + summed.shape[2:])
    me = {axis: lax.axis_index(axis) for axis in GROUP}
    return [
        lax.dynamic_slice(shaped, member(me, offsets) + (0, 0), (1, 1, 1) + shaped.shape[3:])[0, 0, 0]
        for offsets in GROUP_OFFSETS
    ]


def join_slices(lay, blocks, spans, columns):
    rows = blocks[0].shape[0]

    def plan(index):
        copies = []
        for i, offsets in enumerate(GROUP_OFFSETS):
            done = 0
            for start, size in spans(*member(index, offsets)):
                copies.append(
                    (i, (slice(None), pl.ds(done, size)), 0, (slice(None), pl.ds(start, size)))
                )
                done += size
        return copies

    return move(plan, [(rows, columns)], blocks)[0]


def gather_all(lay, block):
    early = None
    for axis in ("t", "a", "u", "c", "b"):
        parts = [block]
        for bit in lay.bits(axis):
            parts = parts + [lay.swap(part, axis, bit) for part in parts]
        block = jnp.stack(parts)
        early = block if axis == "a" else early
    return block.transpose(3, 0, 2, 1, 4, 5, 6), early


def sum_all(lay, value):
    for axis in ("b", "a", "t", "u", "c"):
        for bit in lay.bits(axis):
            value = value + lay.swap(value, axis, bit)
    return value


def dot(left, right):
    return jnp.dot(left, right, preferred_element_type=FULL)


def contract_rows(left, right):
    return lax.dot_general(left, right, (((0,), (0,)), ((), ())), preferred_element_type=FULL)


def contract_cols(left, right):
    return lax.dot_general(left, right, (((1,), (1,)), ((), ())), preferred_element_type=FULL)


def rms_scale(values, gain_row):
    return (
        values
        * lax.rsqrt(jnp.mean(values * values, axis=-1, keepdims=True) + NORM_EPSILON)
        * gain_row
    )


def rms_back(values, gain_row, gradient):
    inverse = lax.rsqrt(jnp.mean(values * values, axis=-1, keepdims=True) + NORM_EPSILON)
    scaled = gradient * gain_row
    along = jnp.mean(values * scaled, axis=-1, keepdims=True)
    value_grad = inverse * scaled - values * (inverse * inverse * inverse * along)
    return value_grad, jnp.sum(gradient * values * inverse, axis=0)


def target_masks(token_ids, clip_ids, frame_ids, context_frames, valid_mask):
    next_ids = jnp.concatenate([token_ids[:, 1:], jnp.zeros_like(token_ids[:, :1])], axis=1)
    never = jnp.zeros_like(clip_ids[:, :1]) > 0
    same_clip = jnp.concatenate([clip_ids[:, 1:] == clip_ids[:, :-1], never], axis=1)
    after_context = jnp.concatenate([frame_ids[:, 1:] > context_frames[:, None], never], axis=1)
    counted = ((valid_mask > 0) & same_clip & after_context).astype(FULL)
    return (next_ids, counted, valid_mask.astype(FULL))


def adam_update(master, moment, variance, gradient, rate, decay):
    new_mean = BETA_FIRST * moment + (1.0 - BETA_FIRST) * gradient
    new_square = BETA_SECOND * variance + (1.0 - BETA_SECOND) * gradient * gradient
    mean_hat = new_mean / (1.0 - BETA_FIRST**STEP)
    square_hat = new_square / (1.0 - BETA_SECOND**STEP)
    new_master = master - rate * (mean_hat / (jnp.sqrt(square_hat) + ADAM_EPSILON) + decay * master)
    return (new_master, new_mean, new_square)


def local(lay, *arguments):
    token_ids, clip_ids, frame_ids, context_frames, valid_mask = arguments[:5]
    masters, moments, variances = arguments[5::3], arguments[6::3], arguments[7::3]
    lookup_half, mixing_half, merging_half, widening_half, narrowing_half, readout_half = (
        master.astype(HALF) for master in masters[:6]
    )
    seqs, length = token_ids.shape
    model_width = lookup_half.shape[1]
    head_size = model_width // HEADS
    me = {axis: lax.axis_index(axis) for axis in ALL}
    me_flat = (((me["u"] * 2 + me["c"]) * lay.a + me["a"]) * 2 + me["t"]) * lay.b + me["b"]

    gain_cols = masters[6].shape[1]
    packed = jnp.concatenate(
        [
            token_ids.astype(FULL).reshape(-1),
            clip_ids.astype(FULL).reshape(-1),
            frame_ids.astype(FULL).reshape(-1),
            valid_mask.astype(FULL).reshape(-1),
            context_frames.astype(FULL),
            lax.reduce_precision(masters[6], 8, 7).reshape(-1),
        ]
    )
    pack_size = packed.shape[0]
    packed = jnp.pad(packed, (0, -pack_size % 1024)).reshape(8, -1)
    everyone, early = gather_all(lay, packed)
    everyone = everyone.reshape(lay.a, lay.b, lay.u, 2, 2, -1)[..., :pack_size]
    flat_all = everyone.reshape(lay.devices, pack_size)
    span = seqs * length

    def unpack(rows):
        ids = [
            rows[:, i * span : (i + 1) * span].reshape(-1, length).astype(jnp.int32) for i in range(4)
        ]
        context = rows[:, 4 * span : 4 * span + seqs].reshape(-1).astype(jnp.int32)
        return ids[0], ids[1], ids[2], context, ids[3]

    _, counted_all, valid_all = target_masks(*unpack(flat_all))
    mask_count, valid_count = jnp.sum(counted_all), jnp.sum(valid_all)
    gains_mine = flat_all[:, 4 * span + seqs :].reshape(lay.devices, 3, gain_cols)
    place_of = jnp.arange(lay.devices)
    rel = place_of ^ me_flat
    rel_t = (rel // lay.b) % 2
    rel_b = rel % lay.b
    rel_a = (rel // (2 * lay.b)) % lay.a
    rel_uc = rel // (2 * lay.a * lay.b)
    spot = ((rel_a * lay.b + rel_b) * lay.u * 2 + rel_uc) * 2 + rel_t
    gain_rows = gains_mine[spot].transpose(1, 0, 2).reshape(3, model_width)

    by_core = everyone[0, 0].transpose(1, 0, 2, 3)
    turned = by_core.transpose(0, 2, 1, 3)
    first_core = me["c"] == 0
    group_rows = jnp.concatenate(
        [
            jnp.where(first_core, turned[0], by_core[0]).reshape(4, pack_size),
            jnp.where(first_core, by_core[1], turned[1]).reshape(4, pack_size),
        ]
    )
    token_g, clip_g, frame_g, context_g, valid_g = unpack(group_rows)
    next_g, counted_g, valid_g = target_masks(token_g, clip_g, frame_g, context_g, valid_g)
    group_seqs = token_g.shape[0]
    flat_tokens, flat_next = token_g.reshape(-1), next_g.reshape(-1)
    counted_flat, valid_flat = counted_g.reshape(-1), valid_g.reshape(-1)
    allowed = (clip_g[:, :, None] == clip_g[:, None, :]) & (
        frame_g[:, None, :] <= frame_g[:, :, None]
    )
    tokens = flat_tokens.shape[0]
    near = tokens // 2

    hidden = narrowing_half.shape[0]
    codes = readout_half.shape[1] // 8

    def mixing_spans(u, c, t):
        return [
            (part * model_width + (((u * 2 + c) * lay.a + a) * 2 + t) * head_size, head_size)
            for part in range(3)
            for a in range(lay.a)
        ]

    def widening_spans(u, c, t):
        size = lay.b * hidden
        return [((((u * 2 + c) * lay.a + a) * 2 + t) * size, size) for a in range(lay.a)]

    def readout_spans(u, c, t):
        return [(((u * 2 + c) * 2 + t) * codes, codes)]

    half_rows = lookup_half.shape[0] // 2
    table_top = Copies(lay, lookup_half[:half_rows], early)
    (mixing_spread,) = spread_slices(lay, [mixing_half], [mixing_spans], early)
    table_low = Copies(lay, lookup_half[half_rows:], [table_top.over_a, mixing_spread])
    widening_spread, readout_spread = spread_slices(
        lay, [widening_half, readout_half], [widening_spans, readout_spans], mixing_spread
    )
    mixing_copies = Copies(lay, mixing_spread, table_low.over_a)
    table = gather_rows(lay, [table_top, table_low])

    table_rows = lookup_half.shape[0]
    row_ids = (
        (((me["u"] * 2 + me["c"]) * lay.a + jnp.arange(lay.a)[:, None, None]) * 2 + me["t"]) * lay.b
        + jnp.arange(lay.b)[None, :, None]
    ) * table_rows + jnp.arange(table_rows)[None, None, :]
    chosen = (flat_tokens[:, None] == row_ids.reshape(1, -1)).astype(HALF)
    chosen_far = after(chosen[near:], [widening_spread, readout_spread])
    embedded = scatter_group(
        lay,
        dot(chosen[:near], table).astype(HALF),
        dot(chosen_far, table).astype(HALF),
        WIRE_HALF,
        None,
        mixing_copies.over_a,
    )
    merging_copies = Copies(lay, merging_half, mixing_copies.over_a)

    normed_one = gather_group(
        lay, rms_scale(embedded, gain_rows[0]).astype(HALF), merging_copies.over_a
    )
    widening_copies = Copies(lay, widening_spread, merging_copies.over_a)
    mixing = gather_slices(lay, mixing_copies)
    merging = gather_rows(lay, [merging_copies])
    joint = dot(normed_one, mixing).astype(HALF)
    heads = joint.reshape(group_seqs, length, 3, lay.a, head_size)
    query_heads, key_heads, value_heads = heads[:, :, 0], heads[:, :, 1], heads[:, :, 2]
    scores = (
        jnp.einsum("bqhd,bkhd->bhqk", query_heads, key_heads, preferred_element_type=FULL)
        * head_size ** (-0.5)
    )
    scores = jnp.where(allowed[:, None], scores, -1e30)
    expo_scores = jnp.exp(scores - jnp.max(scores, axis=-1, keepdims=True))
    attend = expo_scores / jnp.sum(expo_scores, axis=-1, keepdims=True)
    attend_half = attend.astype(HALF)
    mixed_heads = (
        jnp.einsum("bhqk,bkhd->bqhd", attend_half, value_heads, preferred_element_type=FULL)
        .reshape(tokens, -1)
        .astype(HALF)
    )
    mixed_heads = after(mixed_heads, widening_copies.over_a)
    narrowing_copies = Copies(lay, narrowing_half, widening_copies.over_a)
    stream_one = embedded + scatter_group(
        lay, dot(mixed_heads[:near], merging), dot(mixed_heads[near:], merging), WIRE_FORWARD
    )

    normed_two = gather_group(
        lay, rms_scale(stream_one, gain_rows[1]).astype(HALF), narrowing_copies.over_a
    )
    readout_copies = Copies(lay, readout_spread, narrowing_copies.over_a)
    widening = gather_slices(lay, widening_copies)
    narrowing = gather_rows(lay, [narrowing_copies])
    widened = dot(normed_two, widening)
    activated = jax.nn.gelu(widened).astype(HALF)
    stream_two = stream_one + scatter_group(
        lay, dot(activated[:near], narrowing), dot(activated[near:], narrowing), WIRE_FORWARD
    )

    normed_three = gather_group(
        lay, rms_scale(stream_two, gain_rows[2]).astype(HALF), readout_copies.over_a
    )
    readout = gather_slices(lay, readout_copies)
    logits = dot(normed_three, readout)
    code_start = ((me["u"] * 2 + me["c"]) * 2 + me["t"]) * codes
    hit = (code_start + lax.broadcasted_iota(jnp.int32, logits.shape, 1)) == flat_next[:, None]
    top = jnp.max(logits, axis=-1)
    total = jnp.sum(jnp.exp(logits - top[:, None]), axis=-1)
    picked = jnp.sum(jnp.where(hit, logits, 0.0), axis=-1)
    state = jnp.stack([top, total, picked]).reshape(3, 2, 2, 2, -1)
    for stage in range(3):
        if stage == 0:
            other = jnp.flip(lay.swap(state, "c"), axis=1)
        else:
            other = (lay.swap_first, lay.swap_second)[stage - 1](state)
            other = jnp.stack(
                [jnp.flip(other[:, 0], axis=3 - stage), jnp.flip(other[:, 1], axis=stage)], axis=1
            )
        joined = jnp.maximum(state[0], other[0])
        state = jnp.stack(
            [
                joined,
                state[1] * jnp.exp(state[0] - joined) + other[1] * jnp.exp(other[0] - joined),
                state[2] + other[2],
            ]
        )
    top, total, picked = state.reshape(3, tokens)
    log_total = top + jnp.log(total)
    mine = seqs * length
    cross_part = jnp.sum(((log_total - picked) * counted_flat)[:mine])
    square_part = jnp.sum((log_total * log_total * valid_flat)[:mine])
    total_grad = (
        counted_flat / mask_count + 2.0 * SQUARE_COEF * log_total * valid_flat / valid_count
    )
    logit_grad = (
        jnp.exp(logits - log_total[:, None]) * total_grad[:, None]
        - jnp.where(hit, (counted_flat / mask_count)[:, None], 0.0)
    ).astype(HALF)

    readout_red = reduce_slices(lay, contract_rows(normed_three, logit_grad))
    sent = readout_red.prepare()
    normed_three_grad = scatter_group(
        lay,
        contract_cols(logit_grad[:near], readout),
        contract_cols(logit_grad[near:], readout),
        WIRE_BACK,
        sent,
    )
    readout_red.step()
    stream_two_grad, gain_three_grad = rms_back(stream_two, gain_rows[2], normed_three_grad)

    sent = readout_red.prepare()
    branch_grad = gather_group(lay, stream_two_grad.astype(HALF), None, sent)
    _, gelu_pull = jax.vjp(jax.nn.gelu, widened)
    widened_grad = gelu_pull(contract_cols(branch_grad, narrowing))[0].astype(HALF)
    narrowing_red = reduce_rows(lay, contract_rows(activated, branch_grad))
    widening_red = reduce_slices(lay, contract_rows(normed_two, widened_grad))
    sent = narrowing_red.prepare() + widening_red.prepare()
    readout_came = readout_red.step(None, sent)
    normed_two_grad = scatter_group(
        lay,
        contract_cols(widened_grad[:near], widening),
        contract_cols(widened_grad[near:], widening),
        WIRE_BACK,
        sent,
        readout_came,
    )
    narrowing_came = narrowing_red.step()
    widening_came = widening_red.step(narrowing_came)
    stream_one_part, gain_two_grad = rms_back(stream_one, gain_rows[1], normed_two_grad)
    stream_one_grad = stream_two_grad + stream_one_part

    sent = narrowing_red.prepare()
    output_grad = gather_group(lay, stream_one_grad.astype(HALF), None, sent)
    readout_blocks = [
        after(part, output_grad)
        for part in member_blocks(lay, readout_red.finish().astype(SLICE_WIRE))
    ]
    readout_blocks = swap_members(lay, readout_blocks)
    heads_grad = (
        contract_cols(output_grad, merging)
        .astype(HALF)
        .reshape(group_seqs, length, lay.a, head_size)
    )
    value_grad = jnp.einsum(
        "bhqk,bqhd->bkhd", attend_half, heads_grad, preferred_element_type=FULL
    )
    attend_grad = jnp.einsum(
        "bqhd,bkhd->bhqk", heads_grad, value_heads, preferred_element_type=FULL
    )
    score_grad = (
        attend * (attend_grad - jnp.sum(attend_grad * attend, axis=-1, keepdims=True))
    ).astype(HALF)
    head_scale = head_size ** (-0.5)
    query_grad = (
        jnp.einsum("bhqk,bkhd->bqhd", score_grad, key_heads, preferred_element_type=FULL)
        * head_scale
    )
    key_grad = (
        jnp.einsum("bhqk,bqhd->bkhd", score_grad, query_heads, preferred_element_type=FULL)
        * head_scale
    )
    joint_grad = (
        jnp.stack([query_grad, key_grad, value_grad], axis=2).reshape(tokens, -1).astype(HALF)
    )
    mixing_red = reduce_slices(lay, contract_rows(normed_one, joint_grad))
    merging_red = reduce_rows(lay, contract_rows(mixed_heads, output_grad))
    sent = mixing_red.prepare() + merging_red.prepare()
    narrowing_came = narrowing_red.step(None, sent)
    late = [narrowing_came, widening_red.prepare(), readout_blocks]
    normed_one_grad = scatter_group(
        lay,
        contract_cols(joint_grad[:near], mixing),
        contract_cols(joint_grad[near:], mixing),
        WIRE_BACK,
        sent,
        late,
    )
    mixing_came = mixing_red.step()
    merging_red.step(mixing_came)
    embedded_part, gain_one_grad = rms_back(embedded, gain_rows[0], normed_one_grad)
    embedded_grad = stream_one_grad + embedded_part

    sent = mixing_red.prepare() + merging_red.prepare()
    widening_came = widening_red.step(narrowing_came)
    embedded_all = gather_group(lay, embedded_grad.astype(HALF), None, [sent, widening_came])
    mixing_came = mixing_red.step(widening_came)
    lookup_reds = []
    for part in range(2):
        picked_rows = chosen.reshape(tokens, -1, 2, half_rows)[:, :, part].reshape(tokens, -1)
        lookup_reds.append(reduce_rows(lay, contract_rows(picked_rows, embedded_all)))
    sent = [lookup_red.prepare() for lookup_red in lookup_reds]
    widening_blocks = [
        after(part, embedded_all)
        for part in member_blocks(lay, widening_red.finish().astype(SLICE_WIRE))
    ]
    widening_blocks = swap_members(lay, widening_blocks)
    came = [lookup_reds[0].step()]
    came.append(lookup_reds[1].step(came[0]))
    merging_came = merging_red.step(mixing_came)
    lookup_reds[0].prepare()
    lookup_came = lookup_reds[0].step(merging_came)
    lookup_reds[1].prepare()
    lookup_reds[1].step(lookup_came)
    gain_grads = sum_all(lay, jnp.stack([gain_one_grad, gain_two_grad, gain_three_grad]))
    scaling_sum = lax.dynamic_slice(gain_grads, (0, me_flat * gain_cols), (3, gain_cols))
    lookup_sum = jnp.concatenate([lookup_red.finish() for lookup_red in lookup_reds])
    narrowing_sum, merging_sum = narrowing_red.finish(), merging_red.finish()
    readout_sum = join_slices(lay, readout_blocks, readout_spans, readout_half.shape[1])
    widening_sum = join_slices(lay, widening_blocks, widening_spans, widening_half.shape[1])
    mixing_blocks = member_blocks(lay, mixing_red.finish().astype(SLICE_WIRE))
    mixing_blocks = swap_members(lay, mixing_blocks)
    mixing_sum = join_slices(lay, mixing_blocks, mixing_spans, mixing_half.shape[1])

    gradients = [
        to_full(gradient)
        for gradient in (
            lookup_sum,
            mixing_sum,
            merging_sum,
            widening_sum,
            narrowing_sum,
            readout_sum,
            scaling_sum,
        )
    ]
    local_square = sum((jnp.sum(gradient * gradient) for gradient in gradients))
    sums = sum_all(lay, jnp.stack([cross_part, square_part, local_square]))
    norm_value = jnp.sqrt(sums[2])
    clip_factor = jnp.minimum(1.0, CLIP_NORM / norm_value)
    outputs = [jnp.stack([sums[0], mask_count, sums[1], valid_count]), norm_value]
    for index in range(7):
        updated = adam_update(
            masters[index],
            moments[index],
            variances[index],
            gradients[index] * clip_factor,
            LEARN_RATES[index],
            DECAY_RATES[index],
        )
        outputs.extend(updated)
        if index < 6:
            outputs.append(updated[0].astype(HALF))
    return tuple(outputs)


def solution(mesh):
    lay = Layout(mesh)
    row, matrix, columns = P(ALL), P(ALL, None), P(None, ALL)
    in_specs = (matrix, matrix, matrix, row, matrix) + (matrix,) * 18 + (columns,) * 3
    out_specs = (P(), P()) + (matrix,) * 24 + (columns,) * 3
    return jax.shard_map(
        functools.partial(local, lay),
        mesh=lay.mesh,
        in_specs=in_specs,
        out_specs=out_specs,
        check_vma=False,
    )
```

```python
import functools

import jax
import jax.numpy as jnp
from jax import lax
from jax.experimental import pallas as pl
from jax.experimental.pallas import tpu as pltpu
from jax.sharding import Mesh
from jax.sharding import PartitionSpec as P

HEADS = 16
STEP = 5

BETA_FIRST = 0.9
BETA_SECOND = 0.95
ADAM_EPSILON = 1e-08
SQUARE_COEF = 0.01
CLIP_NORM = 0.01
NORM_EPSILON = 1e-05
LEARN_RATES = (0.5, 0.02, 0.02, 0.02, 0.012, 0.02, 0.3)
DECAY_RATES = (0.1, 0.1, 0.1, 0.1, 0.1, 0.1, 0.0)

ALL = ("u", "c", "a", "t", "b")
GROUP = ("u", "c", "t")
HALF = jnp.bfloat16
FULL = jnp.float32
WIRE_HALF = (HALF, HALF, HALF)
WIRE_FORWARD = (HALF, HALF, HALF)
WIRE_BACK = (HALF, HALF, HALF)
SLICE_WIRE = HALF


class Layout:
    def __init__(self, mesh):
        dp, fsdp = mesh.shape["dp"], mesh.shape["fsdp"]
        self.devices = dp * fsdp
        self.b = self.devices // HEADS
        self.a = fsdp // (2 * self.b)
        self.u = dp // 2
        self.mesh = Mesh(mesh.devices.reshape(self.u, 2, self.a, 2, self.b), ALL)
        self.sizes = {"u": self.u, "c": 2, "a": self.a, "t": 2, "b": self.b}

    def swap(self, value, axis, bit=1):
        return lax.ppermute(value, axis, [(i, i ^ bit) for i in range(self.sizes[axis])])

    def swap_group(self, value, ju, jc, jt):
        mask = ju * 4 + jc * 2 + jt
        return lax.ppermute(value, GROUP, [(i, i ^ mask) for i in range(4 * self.u)])

    def swap_first(self, value):
        return lax.ppermute(value, GROUP, [(i, i ^ (1 if i & 2 else 4)) for i in range(4 * self.u)])

    def swap_second(self, value):
        return lax.ppermute(value, GROUP, [(i, i ^ (4 if i & 2 else 1)) for i in range(4 * self.u)])

    def bits(self, axis):
        return [1 << k for k in range(self.sizes[axis].bit_length() - 1)]


def to_full(value):
    return value.astype(FULL)


def after(value, others):
    return value if others is None else lax.optimization_barrier((value, others))[0]


def gather_group(lay, block, middle=None, end=None):
    first, second = after(lay.swap_first(block), middle), lay.swap_second(block)
    near = [block, first, second, lay.swap_second(first)]
    blocks = near + [lay.swap(part, "c") for part in near]
    blocks[-1] = after(blocks[-1], end)
    rows = block.shape[0]

    def plan(index):
        return [(i, None, 0, (pl.ds(i * rows, rows),)) for i in range(8)]

    return move(plan, [(8 * rows, block.shape[1])], blocks)[0]


def scatter_group(lay, near, far, wire, middle=None, end=None):
    rows = near.shape[0] // 4
    half = to_full(near) + to_full(lay.swap(far.astype(wire[0]), "c"))
    second = after(lay.swap_second(half[2 * rows :].astype(wire[1])), middle)
    pair = half[: 2 * rows] + to_full(second)
    first = after(lay.swap_first(pair[rows:].astype(wire[2])), end)
    return pair[:rows] + to_full(first)


class Copies:
    def __init__(self, lay, piece, token):
        piece = after(piece, token)
        self.lay, self.pieces = lay, {(0, 0): piece}
        for bit in lay.bits("a"):
            for key in list(self.pieces):
                self.pieces[key[0] | bit, key[1]] = lay.swap(self.pieces[key], "a", bit)
        self.over_a = [piece for key, piece in self.pieces.items() if key != (0, 0)]

    def finish(self):
        for bit in self.lay.bits("b"):
            for key in list(self.pieces):
                self.pieces[key[0], key[1] | bit] = self.lay.swap(self.pieces[key], "b", bit)
        return self.pieces


class Reduction:
    def __init__(self, lay, pieces):
        self.lay, self.pieces = lay, dict(pieces)
        self.steps = [(axis, bit) for axis in ("b", "a") for bit in reversed(lay.bits(axis))]

    def prepare(self):
        axis, bit = self.steps[0]
        spot = 0 if axis == "a" else 1
        keys = [key for key in self.pieces if key[spot] & bit]
        self.sent = {key: self.pieces.pop(key).astype(HALF) for key in keys}
        return list(self.sent.values())

    def step(self, start=None, end=None):
        axis, bit = self.steps.pop(0)
        came_in = []
        for key, sent in self.sent.items():
            kept = (key[0] ^ bit, key[1]) if axis == "a" else (key[0], key[1] ^ bit)
            came = after(self.lay.swap(after(sent, start), axis, bit), end)
            self.pieces[kept] = to_full(self.pieces[kept]) + to_full(came)
            came_in.append(came)
        return came_in

    def finish(self):
        while self.steps:
            self.prepare()
            self.step()
        return self.pieces[0, 0]


def move_kernel(plan, sources, targets, *refs):
    index = {axis: lax.axis_index(axis) for axis in ALL}
    ins, outs, sems = refs[:sources], refs[sources : sources + targets], refs[sources + targets]
    copies = []
    for number, (source, at_source, target, at_target) in enumerate(plan(index)):
        from_ref = ins[source] if at_source is None else ins[source].at[at_source]
        to_ref = outs[target] if at_target is None else outs[target].at[at_target]
        copies.append(pltpu.make_async_copy(from_ref, to_ref, sems.at[number]))
    for copy in copies:
        copy.start()
    for copy in copies:
        copy.wait()


def move(plan, shapes, sources):
    count = len(plan({axis: 0 for axis in ALL}))
    kind = sources[0].dtype
    return pl.pallas_call(
        functools.partial(move_kernel, plan, len(sources), len(shapes)),
        out_shape=[jax.ShapeDtypeStruct(shape, kind) for shape in shapes],
        in_specs=[pl.BlockSpec(memory_space=pl.ANY)] * len(sources),
        out_specs=[pl.BlockSpec(memory_space=pltpu.VMEM)] * len(shapes),
        scratch_shapes=[pltpu.SemaphoreType.DMA((count,))],
        compiler_params=pltpu.CompilerParams(vmem_limit_bytes=16 * 2**20),
        cost_estimate=pl.CostEstimate(
            flops=0,
            bytes_accessed=2 * sum(s.size * s.dtype.itemsize for s in sources),
            transcendentals=0,
        ),
    )(*sources)


def attention_weights(joint, codes_col, codes_row, head, heads, size):
    query, key, value = (
        joint[:, (part * heads + head) * size : (part * heads + head + 1) * size] for part in range(3)
    )
    allowed = (codes_col[:, 0:1] == codes_row[0:1, :]) & (codes_row[1:2, :] <= codes_col[:, 1:2])
    scores = jnp.where(allowed, contract_cols(query, key) * size ** (-0.5), -1e30)
    expo = jnp.exp(scores - jnp.max(scores, axis=-1, keepdims=True))
    return expo / jnp.sum(expo, axis=-1, keepdims=True), query, key, value


def attention_kernel(heads, size, count, joint_ref, col_ref, row_ref, mixed_ref):
    length = joint_ref.shape[0] // count
    for seq in range(count):
        rows = slice(seq * length, (seq + 1) * length)
        joint = joint_ref[rows, :]
        for head in range(heads):
            attend, _, _, value = attention_weights(
                joint, col_ref[seq], row_ref[seq], head, heads, size
            )
            mixed_ref[rows, head * size : (head + 1) * size] = dot(
                attend.astype(HALF), value
            ).astype(HALF)


def attention_back_kernel(heads, size, count, joint_ref, col_ref, row_ref, grad_ref, out_ref):
    length = joint_ref.shape[0] // count
    for seq in range(count):
        rows = slice(seq * length, (seq + 1) * length)
        joint = joint_ref[rows, :]
        for head in range(heads):
            attend, query, key, value = attention_weights(
                joint, col_ref[seq], row_ref[seq], head, heads, size
            )
            grad = grad_ref[rows, head * size : (head + 1) * size]
            attend_grad = contract_cols(grad, value)
            score_grad = (
                attend * (attend_grad - jnp.sum(attend_grad * attend, axis=-1, keepdims=True))
            ).astype(HALF)
            parts = (
                dot(score_grad, key) * size ** (-0.5),
                contract_rows(score_grad, query) * size ** (-0.5),
                contract_rows(attend.astype(HALF), grad),
            )
            for part, part_grad in enumerate(parts):
                start = (part * heads + head) * size
                out_ref[rows, start : start + size] = part_grad.astype(HALF)


def attention_call(kernel, joint, codes_col, codes_row, more, width, heads, size):
    seqs, length, _ = codes_col.shape
    count = 2 if seqs % 2 == 0 else 1
    wide = [joint] + more
    specs = [pl.BlockSpec((count * length, a.shape[1]), lambda i: (i, 0)) for a in wide]
    code_specs = [
        pl.BlockSpec((count, length, 2), lambda i: (i, 0, 0)),
        pl.BlockSpec((count, 2, length), lambda i: (i, 0, 0)),
    ]
    steps = 2 if kernel is attention_kernel else 6
    return pl.pallas_call(
        functools.partial(kernel, heads, size, count),
        grid=(seqs // count,),
        out_shape=jax.ShapeDtypeStruct((joint.shape[0], width), HALF),
        in_specs=specs[:1] + code_specs + specs[1:],
        out_specs=pl.BlockSpec((count * length, width), lambda i: (i, 0)),
        compiler_params=pltpu.CompilerParams(vmem_limit_bytes=16 * 2**20),
        cost_estimate=pl.CostEstimate(
            flops=2 * steps * seqs * heads * length * length * size,
            bytes_accessed=2 * joint.size * 2,
            transcendentals=seqs * heads * length * length,
        ),
    )(joint, codes_col, codes_row, *more)


GROUP_OFFSETS = [(ju, jc, jt) for ju in (0, 1) for jc in (0, 1) for jt in (0, 1)]


def member(index, offsets):
    return tuple(index[axis] ^ offset for axis, offset in zip(GROUP, offsets))


def swap_members(lay, blocks):
    return list(blocks[:1]) + [
        lay.swap_group(block, *offsets) for block, offsets in zip(blocks[1:], GROUP_OFFSETS[1:])
    ]


def gather_rows(lay, parts):
    pieces = [part.finish() for part in parts]
    rows, width = pieces[0][0, 0].shape
    sources = [(part, key) for part in range(len(parts)) for key in pieces[part]]

    def plan(index):
        return [
            (i, None, 0, (index["a"] ^ ja, index["b"] ^ jb, part))
            for i, (part, (ja, jb)) in enumerate(sources)
        ]

    shape = (lay.a, lay.b, len(parts), rows, width)
    full = move(plan, [shape], [pieces[part][key] for part, key in sources])[0]
    return full.reshape(-1, width)


def spread_slices(lay, shards, spans, start):
    rows = shards[0].shape[0]
    widths = [sum(size for _, size in span(0, 0, 0)) for span in spans]

    def pick(index):
        copies = []
        for i, offsets in enumerate(GROUP_OFFSETS):
            done = 0
            for number, span in enumerate(spans):
                for start, size in span(*member(index, offsets)):
                    copies.append(
                        (number, (slice(None), pl.ds(start, size)), i, (slice(None), pl.ds(done, size)))
                    )
                    done += size
        return copies

    def pile(index):
        copies = []
        for i in range(8):
            done = 0
            for number, width in enumerate(widths):
                copies.append((i, (slice(None), pl.ds(done, width)), number, (i,)))
                done += width
        return copies

    blocks = [after(block, start) for block in move(pick, [(rows, sum(widths))] * 8, shards)]
    received = swap_members(lay, blocks)
    return move(pile, [(8, rows, width) for width in widths], received)


def gather_slices(lay, copies):
    pieces = copies.finish()
    _, rows, width = pieces[0, 0].shape
    keys = list(pieces)

    def plan(index):
        moves = []
        for i, (ja, jb) in enumerate(keys):
            for slot, offsets in enumerate(GROUP_OFFSETS):
                u, c, t = member(index, offsets)
                moves.append((i, (slot,), 0, (u, c, index["a"] ^ ja, t, index["b"] ^ jb)))
        return moves

    shape = (lay.u, 2, lay.a, 2, lay.b, rows, width)
    return move(plan, [shape], [pieces[key] for key in keys])[0].reshape(-1, width)


def reduce_rows(lay, gradient):
    me_a, me_b = lax.axis_index("a"), lax.axis_index("b")
    shaped = gradient.reshape(lay.a, lay.b, -1, gradient.shape[1])
    return Reduction(
        lay,
        {
            (ja, jb): lax.dynamic_slice(
                shaped, (me_a ^ ja, me_b ^ jb, 0, 0), (1, 1) + shaped.shape[2:]
            )[0, 0]
            for ja in range(lay.a)
            for jb in range(lay.b)
        },
    )


def reduce_slices(lay, gradient):
    me_a, me_b = lax.axis_index("a"), lax.axis_index("b")
    width = gradient.shape[1]
    shaped = gradient.reshape(lay.u * 2, lay.a, 2, lay.b, -1, width)
    size = (lay.u * 2, 1, 2, 1, shaped.shape[4], width)
    return Reduction(
        lay,
        {
            (ja, jb): lax.dynamic_slice(shaped, (0, me_a ^ ja, 0, me_b ^ jb, 0, 0), size)[:, 0, :, 0]
            for ja in range(lay.a)
            for jb in range(lay.b)
        },
    )


def member_blocks(lay, summed):
    shaped = summed.reshape((lay.u, 2, 2) + summed.shape[2:])
    me = {axis: lax.axis_index(axis) for axis in GROUP}
    return [
        lax.dynamic_slice(shaped, member(me, offsets) + (0, 0), (1, 1, 1) + shaped.shape[3:])[0, 0, 0]
        for offsets in GROUP_OFFSETS
    ]


def join_slices(lay, blocks, spans, columns):
    rows = blocks[0].shape[0]

    def plan(index):
        copies = []
        for i, offsets in enumerate(GROUP_OFFSETS):
            done = 0
            for start, size in spans(*member(index, offsets)):
                copies.append(
                    (i, (slice(None), pl.ds(done, size)), 0, (slice(None), pl.ds(start, size)))
                )
                done += size
        return copies

    return move(plan, [(rows, columns)], blocks)[0]


def gather_all(lay, block):
    early = None
    for axis in ("t", "a", "u", "c", "b"):
        parts = [block]
        for bit in lay.bits(axis):
            parts = parts + [lay.swap(part, axis, bit) for part in parts]
        block = jnp.stack(parts)
        early = block if axis == "a" else early
    return block.transpose(3, 0, 2, 1, 4, 5, 6), early


def sum_all(lay, value):
    for axis in ("c", "u", "t", "b", "a"):
        for bit in lay.bits(axis):
            value = value + lay.swap(value, axis, bit)
    return value


def dot(left, right):
    return jnp.dot(left, right, preferred_element_type=FULL)


def contract_rows(left, right):
    return lax.dot_general(left, right, (((0,), (0,)), ((), ())), preferred_element_type=FULL)


def contract_cols(left, right):
    return lax.dot_general(left, right, (((1,), (1,)), ((), ())), preferred_element_type=FULL)


def rms_scale(values, gain_row):
    return (
        values
        * lax.rsqrt(jnp.mean(values * values, axis=-1, keepdims=True) + NORM_EPSILON)
        * gain_row
    )


def rms_back(values, gain_row, gradient):
    inverse = lax.rsqrt(jnp.mean(values * values, axis=-1, keepdims=True) + NORM_EPSILON)
    scaled = gradient * gain_row
    along = jnp.mean(values * scaled, axis=-1, keepdims=True)
    value_grad = inverse * scaled - values * (inverse * inverse * inverse * along)
    return value_grad, jnp.sum(gradient * values * inverse, axis=0)


def target_masks(token_ids, clip_ids, frame_ids, context_frames, valid_mask):
    next_ids = jnp.concatenate([token_ids[:, 1:], jnp.zeros_like(token_ids[:, :1])], axis=1)
    never = jnp.zeros_like(clip_ids[:, :1]) > 0
    same_clip = jnp.concatenate([clip_ids[:, 1:] == clip_ids[:, :-1], never], axis=1)
    after_context = jnp.concatenate([frame_ids[:, 1:] > context_frames[:, None], never], axis=1)
    counted = ((valid_mask > 0) & same_clip & after_context).astype(FULL)
    return (next_ids, counted, valid_mask.astype(FULL))


def adam_update(master, moment, variance, gradient, rate, decay):
    new_mean = BETA_FIRST * moment + (1.0 - BETA_FIRST) * gradient
    new_square = BETA_SECOND * variance + (1.0 - BETA_SECOND) * gradient * gradient
    mean_hat = new_mean / (1.0 - BETA_FIRST**STEP)
    square_hat = new_square / (1.0 - BETA_SECOND**STEP)
    new_master = master - rate * (mean_hat / (jnp.sqrt(square_hat) + ADAM_EPSILON) + decay * master)
    return (new_master, new_mean, new_square)


def local(lay, *arguments):
    token_ids, clip_ids, frame_ids, context_frames, valid_mask = arguments[:5]
    masters, moments, variances = arguments[5::3], arguments[6::3], arguments[7::3]
    lookup_half, mixing_half, merging_half, widening_half, narrowing_half, readout_half = (
        master.astype(HALF) for master in masters[:6]
    )
    seqs, length = token_ids.shape
    model_width = lookup_half.shape[1]
    head_size = model_width // HEADS
    me = {axis: lax.axis_index(axis) for axis in ALL}
    me_flat = (((me["u"] * 2 + me["c"]) * lay.a + me["a"]) * 2 + me["t"]) * lay.b + me["b"]

    gain_cols = masters[6].shape[1]
    packed = jnp.concatenate(
        [
            token_ids.astype(FULL).reshape(-1),
            clip_ids.astype(FULL).reshape(-1),
            frame_ids.astype(FULL).reshape(-1),
            valid_mask.astype(FULL).reshape(-1),
            context_frames.astype(FULL),
            lax.reduce_precision(masters[6], 8, 7).reshape(-1),
        ]
    )
    pack_size = packed.shape[0]
    packed = jnp.pad(packed, (0, -pack_size % 1024)).reshape(8, -1)
    everyone, early = gather_all(lay, packed)
    everyone = everyone.reshape(lay.a, lay.b, lay.u, 2, 2, -1)[..., :pack_size]
    flat_all = everyone.reshape(lay.devices, pack_size)
    span = seqs * length

    def unpack(rows):
        ids = [
            rows[:, i * span : (i + 1) * span].reshape(-1, length).astype(jnp.int32) for i in range(4)
        ]
        context = rows[:, 4 * span : 4 * span + seqs].reshape(-1).astype(jnp.int32)
        return ids[0], ids[1], ids[2], context, ids[3]

    _, counted_all, valid_all = target_masks(*unpack(flat_all))
    mask_count, valid_count = jnp.sum(counted_all), jnp.sum(valid_all)
    gains_mine = flat_all[:, 4 * span + seqs :].reshape(lay.devices, 3, gain_cols)
    place_of = jnp.arange(lay.devices)
    rel = place_of ^ me_flat
    rel_t = (rel // lay.b) % 2
    rel_b = rel % lay.b
    rel_a = (rel // (2 * lay.b)) % lay.a
    rel_uc = rel // (2 * lay.a * lay.b)
    spot = ((rel_a * lay.b + rel_b) * lay.u * 2 + rel_uc) * 2 + rel_t
    gain_rows = gains_mine[spot].transpose(1, 0, 2).reshape(3, model_width)

    by_core = everyone[0, 0].transpose(1, 0, 2, 3)
    turned = by_core.transpose(0, 2, 1, 3)
    first_core = me["c"] == 0
    group_rows = jnp.concatenate(
        [
            jnp.where(first_core, turned[0], by_core[0]).reshape(4, pack_size),
            jnp.where(first_core, by_core[1], turned[1]).reshape(4, pack_size),
        ]
    )
    token_g, clip_g, frame_g, context_g, valid_g = unpack(group_rows)
    next_g, counted_g, valid_g = target_masks(token_g, clip_g, frame_g, context_g, valid_g)
    group_seqs = token_g.shape[0]
    flat_tokens, flat_next = token_g.reshape(-1), next_g.reshape(-1)
    counted_flat, valid_flat = counted_g.reshape(-1), valid_g.reshape(-1)
    tokens = flat_tokens.shape[0]
    near = tokens // 2

    hidden = narrowing_half.shape[0]
    code_count = readout_half.shape[1] // 8

    def mixing_spans(u, c, t):
        return [
            (part * model_width + (((u * 2 + c) * lay.a + a) * 2 + t) * head_size, head_size)
            for part in range(3)
            for a in range(lay.a)
        ]

    def widening_spans(u, c, t):
        size = lay.b * hidden
        return [((((u * 2 + c) * lay.a + a) * 2 + t) * size, size) for a in range(lay.a)]

    def readout_spans(u, c, t):
        return [(((u * 2 + c) * 2 + t) * code_count, code_count)]

    half_rows = lookup_half.shape[0] // 2
    table_top = Copies(lay, lookup_half[:half_rows], early)
    (mixing_spread,) = spread_slices(lay, [mixing_half], [mixing_spans], early)
    table_low = Copies(lay, lookup_half[half_rows:], [table_top.over_a, mixing_spread])
    widening_spread, readout_spread = spread_slices(
        lay, [widening_half, readout_half], [widening_spans, readout_spans], mixing_spread
    )
    mixing_copies = Copies(lay, mixing_spread, table_low.over_a)
    table = gather_rows(lay, [table_top, table_low])

    table_rows = lookup_half.shape[0]
    row_ids = (
        (((me["u"] * 2 + me["c"]) * lay.a + jnp.arange(lay.a)[:, None, None]) * 2 + me["t"]) * lay.b
        + jnp.arange(lay.b)[None, :, None]
    ) * table_rows + jnp.arange(table_rows)[None, None, :]
    chosen = (flat_tokens[:, None] == row_ids.reshape(1, -1)).astype(HALF)
    chosen_far = after(chosen[near:], [widening_spread, readout_spread])
    embedded = scatter_group(
        lay,
        dot(chosen[:near], table).astype(HALF),
        dot(chosen_far, table).astype(HALF),
        WIRE_HALF,
        None,
        mixing_copies.over_a,
    )
    merging_copies = Copies(lay, merging_half, mixing_copies.over_a)

    normed_one = gather_group(
        lay, rms_scale(embedded, gain_rows[0]).astype(HALF), merging_copies.over_a
    )
    widening_copies = Copies(lay, widening_spread, merging_copies.over_a)
    mixing = gather_slices(lay, mixing_copies)
    merging = gather_rows(lay, [merging_copies])
    joint = dot(normed_one, mixing).astype(HALF)
    codes = jnp.stack([clip_g, frame_g], axis=1)
    codes_col = codes.transpose(0, 2, 1)
    mixed_heads = attention_call(
        attention_kernel, joint, codes_col, codes, [], merging.shape[0], lay.a, head_size
    )
    mixed_heads = after(mixed_heads, widening_copies.over_a)
    narrowing_copies = Copies(lay, narrowing_half, widening_copies.over_a)
    stream_one = embedded + scatter_group(
        lay, dot(mixed_heads[:near], merging), dot(mixed_heads[near:], merging), WIRE_FORWARD
    )

    normed_two = gather_group(
        lay, rms_scale(stream_one, gain_rows[1]).astype(HALF), narrowing_copies.over_a
    )
    readout_copies = Copies(lay, readout_spread, narrowing_copies.over_a)
    widening = gather_slices(lay, widening_copies)
    narrowing = gather_rows(lay, [narrowing_copies])
    widened = dot(normed_two, widening)
    activated = jax.nn.gelu(widened).astype(HALF)
    stream_two = stream_one + scatter_group(
        lay, dot(activated[:near], narrowing), dot(activated[near:], narrowing), WIRE_FORWARD
    )

    normed_three = gather_group(
        lay, rms_scale(stream_two, gain_rows[2]).astype(HALF), readout_copies.over_a
    )
    readout = gather_slices(lay, readout_copies)
    logits = dot(normed_three, readout)
    code_start = ((me["u"] * 2 + me["c"]) * 2 + me["t"]) * code_count
    hit = (code_start + lax.broadcasted_iota(jnp.int32, logits.shape, 1)) == flat_next[:, None]
    top = jnp.max(logits, axis=-1)
    total = jnp.sum(jnp.exp(logits - top[:, None]), axis=-1)
    picked = jnp.sum(jnp.where(hit, logits, 0.0), axis=-1)
    state = jnp.stack([top, total, picked]).reshape(3, 2, 2, 2, -1)
    for stage in range(3):
        if stage == 0:
            other = jnp.flip(lay.swap(state, "c"), axis=1)
        else:
            other = (lay.swap_first, lay.swap_second)[stage - 1](state)
            other = jnp.stack(
                [jnp.flip(other[:, 0], axis=3 - stage), jnp.flip(other[:, 1], axis=stage)], axis=1
            )
        joined = jnp.maximum(state[0], other[0])
        state = jnp.stack(
            [
                joined,
                state[1] * jnp.exp(state[0] - joined) + other[1] * jnp.exp(other[0] - joined),
                state[2] + other[2],
            ]
        )
    top, total, picked = state.reshape(3, tokens)
    log_total = top + jnp.log(total)
    mine = seqs * length
    cross_part = jnp.sum(((log_total - picked) * counted_flat)[:mine])
    square_part = jnp.sum((log_total * log_total * valid_flat)[:mine])
    total_grad = (
        counted_flat / mask_count + 2.0 * SQUARE_COEF * log_total * valid_flat / valid_count
    )
    logit_grad = (
        jnp.exp(logits - log_total[:, None]) * total_grad[:, None]
        - jnp.where(hit, (counted_flat / mask_count)[:, None], 0.0)
    ).astype(HALF)

    readout_red = reduce_slices(lay, contract_rows(normed_three, logit_grad))
    sent = readout_red.prepare()
    normed_three_grad = scatter_group(
        lay,
        contract_cols(logit_grad[:near], readout),
        contract_cols(logit_grad[near:], readout),
        WIRE_BACK,
        sent,
    )
    readout_red.step()
    stream_two_grad, gain_three_grad = rms_back(stream_two, gain_rows[2], normed_three_grad)

    sent = readout_red.prepare()
    branch_grad = gather_group(lay, stream_two_grad.astype(HALF), None, sent)
    _, gelu_pull = jax.vjp(jax.nn.gelu, widened)
    widened_grad = gelu_pull(contract_cols(branch_grad, narrowing))[0].astype(HALF)
    narrowing_red = reduce_rows(lay, contract_rows(activated, branch_grad))
    widening_red = reduce_slices(lay, contract_rows(normed_two, widened_grad))
    sent = narrowing_red.prepare() + widening_red.prepare()
    readout_came = readout_red.step(None, sent)
    normed_two_grad = scatter_group(
        lay,
        contract_cols(widened_grad[:near], widening),
        contract_cols(widened_grad[near:], widening),
        WIRE_BACK,
        sent,
        readout_came,
    )
    narrowing_red.step()
    widening_red.step()
    stream_one_part, gain_two_grad = rms_back(stream_one, gain_rows[1], normed_two_grad)
    stream_one_grad = stream_two_grad + stream_one_part

    sent = narrowing_red.prepare()
    output_grad = gather_group(lay, stream_one_grad.astype(HALF), None, sent)
    narrowing_came = narrowing_red.step()
    heads_grad = contract_cols(output_grad, merging).astype(HALF)
    joint_grad = attention_call(
        attention_back_kernel, joint, codes_col, codes, [heads_grad], joint.shape[1], lay.a, head_size
    )
    mixing_red = reduce_slices(lay, contract_rows(normed_one, joint_grad))
    merging_red = reduce_rows(lay, contract_rows(mixed_heads, output_grad))
    sent = mixing_red.prepare() + merging_red.prepare()
    late = widening_red.prepare()
    normed_one_grad = scatter_group(
        lay,
        contract_cols(joint_grad[:near], mixing),
        contract_cols(joint_grad[near:], mixing),
        WIRE_BACK,
        sent,
        late,
    )
    widening_came = widening_red.step()
    mixing_red.step()
    merging_red.step()
    embedded_part, gain_one_grad = rms_back(embedded, gain_rows[0], normed_one_grad)
    embedded_grad = stream_one_grad + embedded_part

    sent = mixing_red.prepare() + merging_red.prepare()
    embedded_all = gather_group(
        lay, embedded_grad.astype(HALF), None, [sent, narrowing_came]
    )
    mixing_came = mixing_red.step()
    merging_came = merging_red.step()
    readout_blocks = [
        after(part, embedded_all)
        for part in member_blocks(lay, readout_red.finish().astype(SLICE_WIRE))
    ]
    readout_blocks = swap_members(lay, readout_blocks)
    lookup_reds = []
    for part in range(2):
        picked_rows = chosen.reshape(tokens, -1, 2, half_rows)[:, :, part].reshape(tokens, -1)
        lookup_reds.append(reduce_rows(lay, contract_rows(picked_rows, embedded_all)))
    sent = [lookup_red.prepare() for lookup_red in lookup_reds]
    came = [lookup_red.step() for lookup_red in lookup_reds]
    widening_blocks = [
        after(part, sent)
        for part in member_blocks(lay, widening_red.finish().astype(SLICE_WIRE))
    ]
    widening_blocks = swap_members(lay, widening_blocks)
    mixing_blocks = member_blocks(lay, mixing_red.finish().astype(SLICE_WIRE))
    mixing_blocks = swap_members(lay, mixing_blocks)
    lookup_reds[0].prepare()
    lookup_reds[0].step(None, [widening_blocks, readout_blocks])
    lookup_reds[1].prepare()
    lookup_reds[1].step(None, mixing_blocks)
    gain_grads = jnp.stack([gain_one_grad, gain_two_grad, gain_three_grad])
    gain_grads = sum_all(lay, after(gain_grads, sent))
    scaling_sum = lax.dynamic_slice(gain_grads, (0, me_flat * gain_cols), (3, gain_cols))
    lookup_sum = jnp.concatenate([lookup_red.finish() for lookup_red in lookup_reds])
    narrowing_sum, merging_sum = narrowing_red.finish(), merging_red.finish()
    readout_sum = join_slices(lay, readout_blocks, readout_spans, readout_half.shape[1])
    widening_sum = join_slices(lay, widening_blocks, widening_spans, widening_half.shape[1])
    mixing_sum = join_slices(lay, mixing_blocks, mixing_spans, mixing_half.shape[1])

    gradients = [
        to_full(gradient)
        for gradient in (
            lookup_sum,
            mixing_sum,
            merging_sum,
            widening_sum,
            narrowing_sum,
            readout_sum,
            scaling_sum,
        )
    ]
    local_square = sum((jnp.sum(gradient * gradient) for gradient in gradients))
    sums = sum_all(lay, jnp.stack([cross_part, square_part, local_square]))
    norm_value = jnp.sqrt(sums[2])
    clip_factor = jnp.minimum(1.0, CLIP_NORM / norm_value)
    outputs = [jnp.stack([sums[0], mask_count, sums[1], valid_count]), norm_value]
    for index in range(7):
        updated = adam_update(
            masters[index],
            moments[index],
            variances[index],
            gradients[index] * clip_factor,
            LEARN_RATES[index],
            DECAY_RATES[index],
        )
        outputs.extend(updated)
        if index < 6:
            outputs.append(updated[0].astype(HALF))
    return tuple(outputs)


def solution(mesh):
    lay = Layout(mesh)
    row, matrix, columns = P(ALL), P(ALL, None), P(None, ALL)
    in_specs = (matrix, matrix, matrix, row, matrix) + (matrix,) * 18 + (columns,) * 3
    out_specs = (P(), P()) + (matrix,) * 24 + (columns,) * 3
    return jax.shard_map(
        functools.partial(local, lay),
        mesh=lay.mesh,
        in_specs=in_specs,
        out_specs=out_specs,
        check_vma=False,
    )
```

```python
import functools

import jax
import jax.numpy as jnp
from jax import lax
from jax.experimental import pallas as pl
from jax.experimental.pallas import tpu as pltpu
from jax.sharding import Mesh
from jax.sharding import PartitionSpec as P

HEADS = 16
STEP = 5

BETA_FIRST = 0.9
BETA_SECOND = 0.95
ADAM_EPSILON = 1e-08
SQUARE_COEF = 0.01
CLIP_NORM = 0.01
NORM_EPSILON = 1e-05
LEARN_RATES = (0.5, 0.02, 0.02, 0.02, 0.012, 0.02, 0.3)
DECAY_RATES = (0.1, 0.1, 0.1, 0.1, 0.1, 0.1, 0.0)

ALL = ("u", "c", "a", "t", "b")
GROUP = ("u", "c", "t")
HALF = jnp.bfloat16
FULL = jnp.float32
WIRE_HALF = (HALF, HALF, HALF)
WIRE_FORWARD = (HALF, HALF, HALF)
WIRE_BACK = (HALF, HALF, HALF)
SLICE_WIRE = HALF


class Layout:
    def __init__(self, mesh):
        dp, fsdp = mesh.shape["dp"], mesh.shape["fsdp"]
        self.devices = dp * fsdp
        self.b = self.devices // HEADS
        self.a = fsdp // (2 * self.b)
        self.u = dp // 2
        self.mesh = Mesh(mesh.devices.reshape(self.u, 2, self.a, 2, self.b), ALL)
        self.sizes = {"u": self.u, "c": 2, "a": self.a, "t": 2, "b": self.b}

    def swap(self, value, axis, bit=1):
        return lax.ppermute(value, axis, [(i, i ^ bit) for i in range(self.sizes[axis])])

    def swap_group(self, value, ju, jc, jt):
        mask = ju * 4 + jc * 2 + jt
        return lax.ppermute(value, GROUP, [(i, i ^ mask) for i in range(4 * self.u)])

    def swap_first(self, value):
        return lax.ppermute(value, GROUP, [(i, i ^ (1 if i & 2 else 4)) for i in range(4 * self.u)])

    def swap_second(self, value):
        return lax.ppermute(value, GROUP, [(i, i ^ (4 if i & 2 else 1)) for i in range(4 * self.u)])

    def bits(self, axis):
        return [1 << k for k in range(self.sizes[axis].bit_length() - 1)]


def to_full(value):
    return value.astype(FULL)


def after(value, others):
    return value if others is None else lax.optimization_barrier((value, others))[0]


def gather_group(lay, block, middle=None, end=None):
    first, second = after(lay.swap_first(block), middle), lay.swap_second(block)
    near = [block, first, second, lay.swap_second(first)]
    blocks = near + [lay.swap(part, "c") for part in near]
    blocks[-1] = after(blocks[-1], end)
    rows = block.shape[0]

    def plan(index):
        return [(i, None, 0, (pl.ds(i * rows, rows),)) for i in range(8)]

    return move(plan, [(8 * rows, block.shape[1])], blocks)[0]


def scatter_group(lay, near, far, wire, middle=None, end=None):
    rows = near.shape[0] // 4
    half = to_full(near) + to_full(lay.swap(far.astype(wire[0]), "c"))
    second = after(lay.swap_second(half[2 * rows :].astype(wire[1])), middle)
    pair = half[: 2 * rows] + to_full(second)
    first = after(lay.swap_first(pair[rows:].astype(wire[2])), end)
    return pair[:rows] + to_full(first)


class Copies:
    def __init__(self, lay, piece, token):
        piece = after(piece, token)
        self.lay, self.pieces = lay, {(0, 0): piece}
        for bit in lay.bits("a"):
            for key in list(self.pieces):
                self.pieces[key[0] | bit, key[1]] = lay.swap(self.pieces[key], "a", bit)
        self.cross(lambda key: key[0] == 0)
        self.over_a = [piece for key, piece in self.pieces.items() if key != (0, 0)]

    def cross(self, chosen):
        for bit in self.lay.bits("b"):
            for key in [key for key in self.pieces if chosen(key)]:
                self.pieces[key[0], key[1] | bit] = self.lay.swap(self.pieces[key], "b", bit)

    def finish(self):
        self.cross(lambda key: key[0] > 0)
        return self.pieces


class Reduction:
    def __init__(self, lay, pieces):
        self.lay, self.pieces = lay, dict(pieces)
        self.steps = [(axis, bit) for axis in ("b", "a") for bit in reversed(lay.bits(axis))]

    def prepare(self):
        axis, bit = self.steps[0]
        spot = 0 if axis == "a" else 1
        keys = [key for key in self.pieces if key[spot] & bit]
        self.sent = {key: self.pieces.pop(key).astype(HALF) for key in keys}
        return list(self.sent.values())

    def step(self, start=None, end=None):
        axis, bit = self.steps.pop(0)
        came_in = []
        for key, sent in self.sent.items():
            kept = (key[0] ^ bit, key[1]) if axis == "a" else (key[0], key[1] ^ bit)
            came = after(self.lay.swap(after(sent, start), axis, bit), end)
            self.pieces[kept] = to_full(self.pieces[kept]) + to_full(came)
            came_in.append(came)
        return came_in

    def finish(self):
        while self.steps:
            self.prepare()
            self.step()
        return self.pieces[0, 0]


def move_kernel(plan, sources, targets, *refs):
    index = {axis: lax.axis_index(axis) for axis in ALL}
    ins, outs, sems = refs[:sources], refs[sources : sources + targets], refs[sources + targets]
    copies = []
    for number, (source, at_source, target, at_target) in enumerate(plan(index)):
        from_ref = ins[source] if at_source is None else ins[source].at[at_source]
        to_ref = outs[target] if at_target is None else outs[target].at[at_target]
        copies.append(pltpu.make_async_copy(from_ref, to_ref, sems.at[number]))
    for copy in copies:
        copy.start()
    for copy in copies:
        copy.wait()


def move(plan, shapes, sources):
    count = len(plan({axis: 0 for axis in ALL}))
    kind = sources[0].dtype
    return pl.pallas_call(
        functools.partial(move_kernel, plan, len(sources), len(shapes)),
        out_shape=[jax.ShapeDtypeStruct(shape, kind) for shape in shapes],
        in_specs=[pl.BlockSpec(memory_space=pl.ANY)] * len(sources),
        out_specs=[pl.BlockSpec(memory_space=pltpu.VMEM)] * len(shapes),
        scratch_shapes=[pltpu.SemaphoreType.DMA((count,))],
        compiler_params=pltpu.CompilerParams(vmem_limit_bytes=16 * 2**20),
        cost_estimate=pl.CostEstimate(
            flops=0,
            bytes_accessed=2 * sum(s.size * s.dtype.itemsize for s in sources),
            transcendentals=0,
        ),
    )(*sources)


def attention_weights(joint, codes_col, codes_row, head, heads, size):
    query, key, value = (
        joint[:, (part * heads + head) * size : (part * heads + head + 1) * size] for part in range(3)
    )
    allowed = (codes_col[:, 0:1] == codes_row[0:1, :]) & (codes_row[1:2, :] <= codes_col[:, 1:2])
    scores = jnp.where(allowed, contract_cols(query, key) * size ** (-0.5), -1e30)
    expo = jnp.exp(scores - jnp.max(scores, axis=-1, keepdims=True))
    return expo / jnp.sum(expo, axis=-1, keepdims=True), query, key, value


def attention_kernel(heads, size, count, joint_ref, col_ref, row_ref, mixed_ref):
    length = joint_ref.shape[0] // count
    for seq in range(count):
        rows = slice(seq * length, (seq + 1) * length)
        joint = joint_ref[rows, :]
        for head in range(heads):
            attend, _, _, value = attention_weights(
                joint, col_ref[seq], row_ref[seq], head, heads, size
            )
            mixed_ref[rows, head * size : (head + 1) * size] = dot(
                attend.astype(HALF), value
            ).astype(HALF)


def attention_back_kernel(heads, size, count, joint_ref, col_ref, row_ref, grad_ref, out_ref):
    length = joint_ref.shape[0] // count
    for seq in range(count):
        rows = slice(seq * length, (seq + 1) * length)
        joint = joint_ref[rows, :]
        for head in range(heads):
            attend, query, key, value = attention_weights(
                joint, col_ref[seq], row_ref[seq], head, heads, size
            )
            grad = grad_ref[rows, head * size : (head + 1) * size]
            attend_grad = contract_cols(grad, value)
            score_grad = (
                attend * (attend_grad - jnp.sum(attend_grad * attend, axis=-1, keepdims=True))
            ).astype(HALF)
            parts = (
                dot(score_grad, key) * size ** (-0.5),
                contract_rows(score_grad, query) * size ** (-0.5),
                contract_rows(attend.astype(HALF), grad),
            )
            for part, part_grad in enumerate(parts):
                start = (part * heads + head) * size
                out_ref[rows, start : start + size] = part_grad.astype(HALF)


def attention_call(kernel, joint, codes_col, codes_row, more, width, heads, size):
    seqs, length, _ = codes_col.shape
    count = 2 if seqs % 2 == 0 else 1
    wide = [joint] + more
    specs = [pl.BlockSpec((count * length, a.shape[1]), lambda i: (i, 0)) for a in wide]
    code_specs = [
        pl.BlockSpec((count, length, 2), lambda i: (i, 0, 0)),
        pl.BlockSpec((count, 2, length), lambda i: (i, 0, 0)),
    ]
    steps = 2 if kernel is attention_kernel else 6
    return pl.pallas_call(
        functools.partial(kernel, heads, size, count),
        grid=(seqs // count,),
        out_shape=jax.ShapeDtypeStruct((joint.shape[0], width), HALF),
        in_specs=specs[:1] + code_specs + specs[1:],
        out_specs=pl.BlockSpec((count * length, width), lambda i: (i, 0)),
        compiler_params=pltpu.CompilerParams(vmem_limit_bytes=16 * 2**20),
        cost_estimate=pl.CostEstimate(
            flops=2 * steps * seqs * heads * length * length * size,
            bytes_accessed=2 * joint.size * 2,
            transcendentals=seqs * heads * length * length,
        ),
    )(joint, codes_col, codes_row, *more)


GROUP_OFFSETS = [(ju, jc, jt) for ju in (0, 1) for jc in (0, 1) for jt in (0, 1)]


def member(index, offsets):
    return tuple(index[axis] ^ offset for axis, offset in zip(GROUP, offsets))


def swap_members(lay, blocks):
    return list(blocks[:1]) + [
        lay.swap_group(block, *offsets) for block, offsets in zip(blocks[1:], GROUP_OFFSETS[1:])
    ]


def gather_rows(lay, parts):
    pieces = [part.finish() for part in parts]
    rows, width = pieces[0][0, 0].shape
    sources = [(part, key) for part in range(len(parts)) for key in pieces[part]]

    def plan(index):
        return [
            (i, None, 0, (index["a"] ^ ja, index["b"] ^ jb, part))
            for i, (part, (ja, jb)) in enumerate(sources)
        ]

    shape = (lay.a, lay.b, len(parts), rows, width)
    full = move(plan, [shape], [pieces[part][key] for part, key in sources])[0]
    return full.reshape(-1, width)


def spread_slices(lay, shards, spans, start):
    rows = shards[0].shape[0]
    widths = [sum(size for _, size in span(0, 0, 0)) for span in spans]

    def pick(index):
        copies = []
        for i, offsets in enumerate(GROUP_OFFSETS):
            done = 0
            for number, span in enumerate(spans):
                for start, size in span(*member(index, offsets)):
                    copies.append(
                        (number, (slice(None), pl.ds(start, size)), i, (slice(None), pl.ds(done, size)))
                    )
                    done += size
        return copies

    def pile(index):
        copies = []
        for i in range(8):
            done = 0
            for number, width in enumerate(widths):
                copies.append((i, (slice(None), pl.ds(done, width)), number, (i,)))
                done += width
        return copies

    blocks = [after(block, start) for block in move(pick, [(rows, sum(widths))] * 8, shards)]
    received = swap_members(lay, blocks)
    return move(pile, [(8, rows, width) for width in widths], received)


def gather_slices(lay, copies):
    pieces = copies.finish()
    _, rows, width = pieces[0, 0].shape
    keys = list(pieces)

    def plan(index):
        moves = []
        for i, (ja, jb) in enumerate(keys):
            for slot, offsets in enumerate(GROUP_OFFSETS):
                u, c, t = member(index, offsets)
                moves.append((i, (slot,), 0, (u, c, index["a"] ^ ja, t, index["b"] ^ jb)))
        return moves

    shape = (lay.u, 2, lay.a, 2, lay.b, rows, width)
    return move(plan, [shape], [pieces[key] for key in keys])[0].reshape(-1, width)


def reduce_rows(lay, gradient):
    me_a, me_b = lax.axis_index("a"), lax.axis_index("b")
    shaped = gradient.reshape(lay.a, lay.b, -1, gradient.shape[1])
    return Reduction(
        lay,
        {
            (ja, jb): lax.dynamic_slice(
                shaped, (me_a ^ ja, me_b ^ jb, 0, 0), (1, 1) + shaped.shape[2:]
            )[0, 0]
            for ja in range(lay.a)
            for jb in range(lay.b)
        },
    )


def reduce_slices(lay, gradient):
    me_a, me_b = lax.axis_index("a"), lax.axis_index("b")
    width = gradient.shape[1]
    shaped = gradient.reshape(lay.u * 2, lay.a, 2, lay.b, -1, width)
    size = (lay.u * 2, 1, 2, 1, shaped.shape[4], width)
    return Reduction(
        lay,
        {
            (ja, jb): lax.dynamic_slice(shaped, (0, me_a ^ ja, 0, me_b ^ jb, 0, 0), size)[:, 0, :, 0]
            for ja in range(lay.a)
            for jb in range(lay.b)
        },
    )


def member_blocks(lay, summed):
    shaped = summed.reshape((lay.u, 2, 2) + summed.shape[2:])
    me = {axis: lax.axis_index(axis) for axis in GROUP}
    return [
        lax.dynamic_slice(shaped, member(me, offsets) + (0, 0), (1, 1, 1) + shaped.shape[3:])[0, 0, 0]
        for offsets in GROUP_OFFSETS
    ]


def join_slices(lay, blocks, spans, columns):
    rows = blocks[0].shape[0]

    def plan(index):
        copies = []
        for i, offsets in enumerate(GROUP_OFFSETS):
            done = 0
            for start, size in spans(*member(index, offsets)):
                copies.append(
                    (i, (slice(None), pl.ds(done, size)), 0, (slice(None), pl.ds(start, size)))
                )
                done += size
        return copies

    return move(plan, [(rows, columns)], blocks)[0]


def gather_all(lay, block):
    early = None
    for axis in ("t", "a", "u", "c", "b"):
        parts = [block]
        for bit in lay.bits(axis):
            parts = parts + [lay.swap(part, axis, bit) for part in parts]
        block = jnp.stack(parts)
        early = block if axis == "a" else early
    return block.transpose(3, 0, 2, 1, 4, 5, 6), early


def sum_all(lay, value):
    for axis in ("c", "u", "t", "b", "a"):
        for bit in lay.bits(axis):
            value = value + lay.swap(value, axis, bit)
    return value


def dot(left, right):
    return jnp.dot(left, right, preferred_element_type=FULL)


def contract_rows(left, right):
    return lax.dot_general(left, right, (((0,), (0,)), ((), ())), preferred_element_type=FULL)


def contract_cols(left, right):
    return lax.dot_general(left, right, (((1,), (1,)), ((), ())), preferred_element_type=FULL)


def rms_scale(values, gain_row):
    return (
        values
        * lax.rsqrt(jnp.mean(values * values, axis=-1, keepdims=True) + NORM_EPSILON)
        * gain_row
    )


def rms_back(values, gain_row, gradient):
    inverse = lax.rsqrt(jnp.mean(values * values, axis=-1, keepdims=True) + NORM_EPSILON)
    scaled = gradient * gain_row
    along = jnp.mean(values * scaled, axis=-1, keepdims=True)
    value_grad = inverse * scaled - values * (inverse * inverse * inverse * along)
    return value_grad, jnp.sum(gradient * values * inverse, axis=0)


def target_masks(token_ids, clip_ids, frame_ids, context_frames, valid_mask):
    next_ids = jnp.concatenate([token_ids[:, 1:], jnp.zeros_like(token_ids[:, :1])], axis=1)
    never = jnp.zeros_like(clip_ids[:, :1]) > 0
    same_clip = jnp.concatenate([clip_ids[:, 1:] == clip_ids[:, :-1], never], axis=1)
    after_context = jnp.concatenate([frame_ids[:, 1:] > context_frames[:, None], never], axis=1)
    counted = ((valid_mask > 0) & same_clip & after_context).astype(FULL)
    return (next_ids, counted, valid_mask.astype(FULL))


def adam_update(master, moment, variance, gradient, rate, decay):
    new_mean = BETA_FIRST * moment + (1.0 - BETA_FIRST) * gradient
    new_square = BETA_SECOND * variance + (1.0 - BETA_SECOND) * gradient * gradient
    mean_hat = new_mean / (1.0 - BETA_FIRST**STEP)
    square_hat = new_square / (1.0 - BETA_SECOND**STEP)
    new_master = master - rate * (mean_hat / (jnp.sqrt(square_hat) + ADAM_EPSILON) + decay * master)
    return (new_master, new_mean, new_square)


def local(lay, *arguments):
    token_ids, clip_ids, frame_ids, context_frames, valid_mask = arguments[:5]
    masters, moments, variances = arguments[5::3], arguments[6::3], arguments[7::3]
    lookup_half, mixing_half, merging_half, widening_half, narrowing_half, readout_half = (
        master.astype(HALF) for master in masters[:6]
    )
    seqs, length = token_ids.shape
    model_width = lookup_half.shape[1]
    head_size = model_width // HEADS
    me = {axis: lax.axis_index(axis) for axis in ALL}
    me_flat = (((me["u"] * 2 + me["c"]) * lay.a + me["a"]) * 2 + me["t"]) * lay.b + me["b"]

    gain_cols = masters[6].shape[1]
    packed = jnp.concatenate(
        [
            token_ids.astype(FULL).reshape(-1),
            clip_ids.astype(FULL).reshape(-1),
            frame_ids.astype(FULL).reshape(-1),
            valid_mask.astype(FULL).reshape(-1),
            context_frames.astype(FULL),
            lax.reduce_precision(masters[6], 8, 7).reshape(-1),
        ]
    )
    pack_size = packed.shape[0]
    packed = jnp.pad(packed, (0, -pack_size % 1024)).reshape(8, -1)
    everyone, early = gather_all(lay, packed)
    everyone = everyone.reshape(lay.a, lay.b, lay.u, 2, 2, -1)[..., :pack_size]
    flat_all = everyone.reshape(lay.devices, pack_size)
    span = seqs * length

    def unpack(rows):
        ids = [
            rows[:, i * span : (i + 1) * span].reshape(-1, length).astype(jnp.int32) for i in range(4)
        ]
        context = rows[:, 4 * span : 4 * span + seqs].reshape(-1).astype(jnp.int32)
        return ids[0], ids[1], ids[2], context, ids[3]

    _, counted_all, valid_all = target_masks(*unpack(flat_all))
    mask_count, valid_count = jnp.sum(counted_all), jnp.sum(valid_all)
    gains_mine = flat_all[:, 4 * span + seqs :].reshape(lay.devices, 3, gain_cols)
    place_of = jnp.arange(lay.devices)
    rel = place_of ^ me_flat
    rel_t = (rel // lay.b) % 2
    rel_b = rel % lay.b
    rel_a = (rel // (2 * lay.b)) % lay.a
    rel_uc = rel // (2 * lay.a * lay.b)
    spot = ((rel_a * lay.b + rel_b) * lay.u * 2 + rel_uc) * 2 + rel_t
    gain_rows = gains_mine[spot].transpose(1, 0, 2).reshape(3, model_width)

    by_core = everyone[0, 0].transpose(1, 0, 2, 3)
    turned = by_core.transpose(0, 2, 1, 3)
    first_core = me["c"] == 0
    group_rows = jnp.concatenate(
        [
            jnp.where(first_core, turned[0], by_core[0]).reshape(4, pack_size),
            jnp.where(first_core, by_core[1], turned[1]).reshape(4, pack_size),
        ]
    )
    token_g, clip_g, frame_g, context_g, valid_g = unpack(group_rows)
    next_g, counted_g, valid_g = target_masks(token_g, clip_g, frame_g, context_g, valid_g)
    group_seqs = token_g.shape[0]
    flat_tokens, flat_next = token_g.reshape(-1), next_g.reshape(-1)
    counted_flat, valid_flat = counted_g.reshape(-1), valid_g.reshape(-1)
    tokens = flat_tokens.shape[0]
    near = tokens // 2

    hidden = narrowing_half.shape[0]
    code_count = readout_half.shape[1] // 8

    def mixing_spans(u, c, t):
        return [
            (part * model_width + (((u * 2 + c) * lay.a + a) * 2 + t) * head_size, head_size)
            for part in range(3)
            for a in range(lay.a)
        ]

    def widening_spans(u, c, t):
        size = lay.b * hidden
        return [((((u * 2 + c) * lay.a + a) * 2 + t) * size, size) for a in range(lay.a)]

    def readout_spans(u, c, t):
        return [(((u * 2 + c) * 2 + t) * code_count, code_count)]

    half_rows = lookup_half.shape[0] // 2
    table_top = Copies(lay, lookup_half[:half_rows], early)
    (mixing_spread,) = spread_slices(lay, [mixing_half], [mixing_spans], early)
    table_low = Copies(lay, lookup_half[half_rows:], [table_top.over_a, mixing_spread])
    widening_spread, readout_spread = spread_slices(
        lay, [widening_half, readout_half], [widening_spans, readout_spans], mixing_spread
    )
    mixing_copies = Copies(lay, mixing_spread, table_low.over_a)
    table = gather_rows(lay, [table_top, table_low])

    table_rows = lookup_half.shape[0]
    row_ids = (
        (((me["u"] * 2 + me["c"]) * lay.a + jnp.arange(lay.a)[:, None, None]) * 2 + me["t"]) * lay.b
        + jnp.arange(lay.b)[None, :, None]
    ) * table_rows + jnp.arange(table_rows)[None, None, :]
    chosen = (flat_tokens[:, None] == row_ids.reshape(1, -1)).astype(HALF)
    chosen_far = after(chosen[near:], [widening_spread, readout_spread])
    embedded = scatter_group(
        lay,
        dot(chosen[:near], table).astype(HALF),
        dot(chosen_far, table).astype(HALF),
        WIRE_HALF,
        None,
        mixing_copies.over_a,
    )
    merging_copies = Copies(lay, merging_half, mixing_copies.over_a)

    normed_one = gather_group(
        lay, rms_scale(embedded, gain_rows[0]).astype(HALF), merging_copies.over_a
    )
    widening_copies = Copies(lay, widening_spread, merging_copies.over_a)
    mixing = gather_slices(lay, mixing_copies)
    merging = gather_rows(lay, [merging_copies])
    joint = dot(normed_one, mixing).astype(HALF)
    codes = jnp.stack([clip_g, frame_g], axis=1)
    codes_col = codes.transpose(0, 2, 1)
    mixed_heads = attention_call(
        attention_kernel, joint, codes_col, codes, [], merging.shape[0], lay.a, head_size
    )
    narrowing_copies = Copies(lay, narrowing_half, widening_copies.over_a)
    stream_one = embedded + scatter_group(
        lay,
        dot(mixed_heads[:near], merging),
        dot(mixed_heads[near:], merging),
        WIRE_FORWARD,
        widening_copies.over_a,
    )

    normed_two = gather_group(
        lay, rms_scale(stream_one, gain_rows[1]).astype(HALF), narrowing_copies.over_a
    )
    readout_copies = Copies(lay, readout_spread, narrowing_copies.over_a)
    widening = gather_slices(lay, widening_copies)
    narrowing = gather_rows(lay, [narrowing_copies])
    widened = dot(normed_two, widening)
    activated = jax.nn.gelu(widened).astype(HALF)
    stream_two = stream_one + scatter_group(
        lay, dot(activated[:near], narrowing), dot(activated[near:], narrowing), WIRE_FORWARD
    )

    normed_three = gather_group(
        lay, rms_scale(stream_two, gain_rows[2]).astype(HALF), readout_copies.over_a
    )
    readout = gather_slices(lay, readout_copies)
    logits = dot(normed_three, readout)
    code_start = ((me["u"] * 2 + me["c"]) * 2 + me["t"]) * code_count
    hit = (code_start + lax.broadcasted_iota(jnp.int32, logits.shape, 1)) == flat_next[:, None]
    top = jnp.max(logits, axis=-1)
    total = jnp.sum(jnp.exp(logits - top[:, None]), axis=-1)
    picked = jnp.sum(jnp.where(hit, logits, 0.0), axis=-1)
    state = jnp.stack([top, total, picked]).reshape(3, 2, 2, 2, -1)
    for stage in range(3):
        if stage == 0:
            other = jnp.flip(lay.swap(state, "c"), axis=1)
        else:
            other = (lay.swap_first, lay.swap_second)[stage - 1](state)
            other = jnp.stack(
                [jnp.flip(other[:, 0], axis=3 - stage), jnp.flip(other[:, 1], axis=stage)], axis=1
            )
        joined = jnp.maximum(state[0], other[0])
        state = jnp.stack(
            [
                joined,
                state[1] * jnp.exp(state[0] - joined) + other[1] * jnp.exp(other[0] - joined),
                state[2] + other[2],
            ]
        )
    top, total, picked = state.reshape(3, tokens)
    log_total = top + jnp.log(total)
    mine = seqs * length
    cross_part = jnp.sum(((log_total - picked) * counted_flat)[:mine])
    square_part = jnp.sum((log_total * log_total * valid_flat)[:mine])
    total_grad = (
        counted_flat / mask_count + 2.0 * SQUARE_COEF * log_total * valid_flat / valid_count
    )
    logit_grad = (
        jnp.exp(logits - log_total[:, None]) * total_grad[:, None]
        - jnp.where(hit, (counted_flat / mask_count)[:, None], 0.0)
    ).astype(HALF)

    readout_red = reduce_slices(lay, contract_rows(normed_three, logit_grad))
    sent = readout_red.prepare()
    normed_three_grad = scatter_group(
        lay,
        contract_cols(logit_grad[:near], readout),
        contract_cols(logit_grad[near:], readout),
        WIRE_BACK,
        sent,
    )
    readout_red.step()
    stream_two_grad, gain_three_grad = rms_back(stream_two, gain_rows[2], normed_three_grad)

    sent = readout_red.prepare()
    branch_grad = gather_group(lay, stream_two_grad.astype(HALF), None, sent)
    _, gelu_pull = jax.vjp(jax.nn.gelu, widened)
    widened_grad = gelu_pull(contract_cols(branch_grad, narrowing))[0].astype(HALF)
    narrowing_red = reduce_rows(lay, contract_rows(activated, branch_grad))
    widening_red = reduce_slices(lay, contract_rows(normed_two, widened_grad))
    sent = narrowing_red.prepare() + widening_red.prepare()
    readout_came = readout_red.step(None, sent)
    normed_two_grad = scatter_group(
        lay,
        contract_cols(widened_grad[:near], widening),
        contract_cols(widened_grad[near:], widening),
        WIRE_BACK,
        sent,
        readout_came,
    )
    narrowing_red.step()
    widening_red.step()
    stream_one_part, gain_two_grad = rms_back(stream_one, gain_rows[1], normed_two_grad)
    stream_one_grad = stream_two_grad + stream_one_part

    sent = narrowing_red.prepare()
    output_grad = gather_group(lay, stream_one_grad.astype(HALF), None, sent)
    narrowing_came = narrowing_red.step()
    heads_grad = contract_cols(output_grad, merging).astype(HALF)
    joint_grad = attention_call(
        attention_back_kernel, joint, codes_col, codes, [heads_grad], joint.shape[1], lay.a, head_size
    )
    mixing_red = reduce_slices(lay, contract_rows(normed_one, joint_grad))
    merging_red = reduce_rows(lay, contract_rows(mixed_heads, output_grad))
    sent = mixing_red.prepare() + merging_red.prepare()
    late = widening_red.prepare()
    normed_one_grad = scatter_group(
        lay,
        contract_cols(joint_grad[:near], mixing),
        contract_cols(joint_grad[near:], mixing),
        WIRE_BACK,
        sent,
        late,
    )
    widening_came = widening_red.step()
    mixing_red.step()
    merging_red.step()
    embedded_part, gain_one_grad = rms_back(embedded, gain_rows[0], normed_one_grad)
    embedded_grad = stream_one_grad + embedded_part

    sent = mixing_red.prepare() + merging_red.prepare()
    embedded_all = gather_group(
        lay, embedded_grad.astype(HALF), None, [sent, narrowing_came]
    )
    mixing_came = mixing_red.step()
    merging_came = merging_red.step()
    readout_blocks = [
        after(part, embedded_all)
        for part in member_blocks(lay, readout_red.finish().astype(SLICE_WIRE))
    ]
    readout_blocks = swap_members(lay, readout_blocks)
    lookup_reds = []
    for part in range(2):
        picked_rows = chosen.reshape(tokens, -1, 2, half_rows)[:, :, part].reshape(tokens, -1)
        lookup_reds.append(reduce_rows(lay, contract_rows(picked_rows, embedded_all)))
    sent = [lookup_red.prepare() for lookup_red in lookup_reds]
    came = [lookup_red.step() for lookup_red in lookup_reds]
    widening_blocks = [
        after(part, sent)
        for part in member_blocks(lay, widening_red.finish().astype(SLICE_WIRE))
    ]
    widening_blocks = swap_members(lay, widening_blocks)
    mixing_blocks = member_blocks(lay, mixing_red.finish().astype(SLICE_WIRE))
    mixing_blocks = swap_members(lay, mixing_blocks)
    lookup_reds[0].prepare()
    lookup_reds[0].step(None, [widening_blocks, readout_blocks])
    lookup_reds[1].prepare()
    lookup_reds[1].step(None, mixing_blocks)
    gain_grads = jnp.stack([gain_one_grad, gain_two_grad, gain_three_grad])
    gain_grads = sum_all(lay, after(gain_grads, sent))
    scaling_sum = lax.dynamic_slice(gain_grads, (0, me_flat * gain_cols), (3, gain_cols))
    lookup_sum = jnp.concatenate([lookup_red.finish() for lookup_red in lookup_reds])
    narrowing_sum, merging_sum = narrowing_red.finish(), merging_red.finish()
    readout_sum = join_slices(lay, readout_blocks, readout_spans, readout_half.shape[1])
    widening_sum = join_slices(lay, widening_blocks, widening_spans, widening_half.shape[1])
    mixing_sum = join_slices(lay, mixing_blocks, mixing_spans, mixing_half.shape[1])

    gradients = [
        to_full(gradient)
        for gradient in (
            lookup_sum,
            mixing_sum,
            merging_sum,
            widening_sum,
            narrowing_sum,
            readout_sum,
            scaling_sum,
        )
    ]
    local_square = sum((jnp.sum(gradient * gradient) for gradient in gradients))
    sums = sum_all(lay, jnp.stack([cross_part, square_part, local_square]))
    norm_value = jnp.sqrt(sums[2])
    clip_factor = jnp.minimum(1.0, CLIP_NORM / norm_value)
    outputs = [jnp.stack([sums[0], mask_count, sums[1], valid_count]), norm_value]
    for index in range(7):
        updated = adam_update(
            masters[index],
            moments[index],
            variances[index],
            gradients[index] * clip_factor,
            LEARN_RATES[index],
            DECAY_RATES[index],
        )
        outputs.extend(updated)
        if index < 6:
            outputs.append(updated[0].astype(HALF))
    return tuple(outputs)


def solution(mesh):
    lay = Layout(mesh)
    row, matrix, columns = P(ALL), P(ALL, None), P(None, ALL)
    in_specs = (matrix, matrix, matrix, row, matrix) + (matrix,) * 18 + (columns,) * 3
    out_specs = (P(), P()) + (matrix,) * 24 + (columns,) * 3
    return jax.shard_map(
        functools.partial(local, lay),
        mesh=lay.mesh,
        in_specs=in_specs,
        out_specs=out_specs,
        check_vma=False,
    )
```

```python
import functools

import jax
import jax.numpy as jnp
from jax import lax
from jax.experimental import pallas as pl
from jax.experimental.pallas import tpu as pltpu
from jax.sharding import Mesh
from jax.sharding import PartitionSpec as P

HEADS = 16
STEP = 5

BETA_FIRST = 0.9
BETA_SECOND = 0.95
ADAM_EPSILON = 1e-08
SQUARE_COEF = 0.01
CLIP_NORM = 0.01
NORM_EPSILON = 1e-05
LEARN_RATES = (0.5, 0.02, 0.02, 0.02, 0.012, 0.02, 0.3)
DECAY_RATES = (0.1, 0.1, 0.1, 0.1, 0.1, 0.1, 0.0)

ALL = ("u", "c", "a", "t", "b")
GROUP = ("u", "c", "t")
HALF = jnp.bfloat16
FULL = jnp.float32
WIRE_HALF = (HALF, HALF, HALF)
WIRE_FORWARD = (HALF, HALF, HALF)
WIRE_BACK = (HALF, HALF, HALF)
SLICE_WIRE = HALF


class Layout:
    def __init__(self, mesh):
        dp, fsdp = mesh.shape["dp"], mesh.shape["fsdp"]
        self.devices = dp * fsdp
        self.b = self.devices // HEADS
        self.a = fsdp // (2 * self.b)
        self.u = dp // 2
        self.mesh = Mesh(mesh.devices.reshape(self.u, 2, self.a, 2, self.b), ALL)
        self.sizes = {"u": self.u, "c": 2, "a": self.a, "t": 2, "b": self.b}

    def swap(self, value, axis, bit=1):
        return lax.ppermute(value, axis, [(i, i ^ bit) for i in range(self.sizes[axis])])

    def swap_group(self, value, ju, jc, jt):
        mask = ju * 4 + jc * 2 + jt
        return lax.ppermute(value, GROUP, [(i, i ^ mask) for i in range(4 * self.u)])

    def swap_first(self, value):
        return lax.ppermute(value, GROUP, [(i, i ^ (1 if i & 2 else 4)) for i in range(4 * self.u)])

    def swap_second(self, value):
        return lax.ppermute(value, GROUP, [(i, i ^ (4 if i & 2 else 1)) for i in range(4 * self.u)])

    def bits(self, axis):
        return [1 << k for k in range(self.sizes[axis].bit_length() - 1)]


def to_full(value):
    return value.astype(FULL)


def after(value, others):
    return value if others is None else lax.optimization_barrier((value, others))[0]


def gather_group(lay, block, middle=None, end=None):
    first, second = after(lay.swap_first(block), middle), lay.swap_second(block)
    near = [block, first, second, lay.swap_second(first)]
    blocks = near + [lay.swap(part, "c") for part in near]
    blocks[-1] = after(blocks[-1], end)
    rows = block.shape[0]

    def plan(index):
        return [(i, None, 0, (pl.ds(i * rows, rows),)) for i in range(8)]

    return move(plan, [(8 * rows, block.shape[1])], blocks)[0]


def scatter_group(lay, left, product, wire, middle=None, end=None):
    rows = left.shape[0] // 8

    def over_cores(start):
        far = product(left[(start + 4) * rows : (start + 6) * rows]).astype(wire[0])
        near = product(left[start * rows : (start + 2) * rows])
        return near + to_full(lay.swap(far, "c"))

    late = over_cores(2).astype(wire[1])
    both = lay.swap_second(late[rows:])
    early = over_cores(0)
    first = after(lay.swap_first((early[rows:] + to_full(both)).astype(wire[2])), end)
    second = after(lay.swap_second(late[:rows]), middle)
    return early[:rows] + to_full(second) + to_full(first)


class Copies:
    def __init__(self, lay, piece, token):
        piece = after(piece, token)
        self.lay, self.pieces = lay, {(0, 0): piece}
        for bit in lay.bits("a"):
            for key in list(self.pieces):
                self.pieces[key[0] | bit, key[1]] = lay.swap(self.pieces[key], "a", bit)
        self.cross(lambda key: key[0] == 0)
        self.over_a = [piece for key, piece in self.pieces.items() if key != (0, 0)]

    def cross(self, chosen):
        for bit in self.lay.bits("b"):
            for key in [key for key in self.pieces if chosen(key)]:
                self.pieces[key[0], key[1] | bit] = self.lay.swap(self.pieces[key], "b", bit)

    def finish(self):
        self.cross(lambda key: key[0] > 0)
        return self.pieces


class Reduction:
    def __init__(self, lay, pieces):
        self.lay, self.pieces = lay, dict(pieces)
        self.steps = [(axis, bit) for axis in ("b", "a") for bit in reversed(lay.bits(axis))]

    def prepare(self):
        axis, bit = self.steps[0]
        spot = 0 if axis == "a" else 1
        keys = [key for key in self.pieces if key[spot] & bit]
        self.sent = {key: self.pieces.pop(key).astype(HALF) for key in keys}
        return list(self.sent.values())

    def step(self, start=None, end=None):
        axis, bit = self.steps.pop(0)
        came_in = []
        for key, sent in self.sent.items():
            kept = (key[0] ^ bit, key[1]) if axis == "a" else (key[0], key[1] ^ bit)
            came = after(self.lay.swap(after(sent, start), axis, bit), end)
            self.pieces[kept] = to_full(self.pieces[kept]) + to_full(came)
            came_in.append(came)
        return came_in

    def finish(self):
        while self.steps:
            self.prepare()
            self.step()
        return self.pieces[0, 0]


def move_kernel(plan, sources, targets, *refs):
    index = {axis: lax.axis_index(axis) for axis in ALL}
    ins, outs, sems = refs[:sources], refs[sources : sources + targets], refs[sources + targets]
    copies = []
    for number, (source, at_source, target, at_target) in enumerate(plan(index)):
        from_ref = ins[source] if at_source is None else ins[source].at[at_source]
        to_ref = outs[target] if at_target is None else outs[target].at[at_target]
        copies.append(pltpu.make_async_copy(from_ref, to_ref, sems.at[number]))
    for copy in copies:
        copy.start()
    for copy in copies:
        copy.wait()


def move(plan, shapes, sources):
    count = len(plan({axis: 0 for axis in ALL}))
    kind = sources[0].dtype
    return pl.pallas_call(
        functools.partial(move_kernel, plan, len(sources), len(shapes)),
        out_shape=[jax.ShapeDtypeStruct(shape, kind) for shape in shapes],
        in_specs=[pl.BlockSpec(memory_space=pl.ANY)] * len(sources),
        out_specs=[pl.BlockSpec(memory_space=pltpu.VMEM)] * len(shapes),
        scratch_shapes=[pltpu.SemaphoreType.DMA((count,))],
        compiler_params=pltpu.CompilerParams(vmem_limit_bytes=16 * 2**20),
        cost_estimate=pl.CostEstimate(
            flops=0,
            bytes_accessed=2 * sum(s.size * s.dtype.itemsize for s in sources),
            transcendentals=0,
        ),
    )(*sources)


def attention_weights(joint, codes_col, codes_row, head, heads, size):
    query, key, value = (
        joint[:, (part * heads + head) * size : (part * heads + head + 1) * size] for part in range(3)
    )
    allowed = (codes_col[:, 0:1] == codes_row[0:1, :]) & (codes_row[1:2, :] <= codes_col[:, 1:2])
    scores = jnp.where(allowed, contract_cols(query, key) * size ** (-0.5), -1e30)
    expo = jnp.exp(scores - jnp.max(scores, axis=-1, keepdims=True))
    return expo / jnp.sum(expo, axis=-1, keepdims=True), query, key, value


def attention_kernel(heads, size, count, joint_ref, col_ref, row_ref, mixed_ref):
    length = joint_ref.shape[0] // count
    for seq in range(count):
        rows = slice(seq * length, (seq + 1) * length)
        joint = joint_ref[rows, :]
        for head in range(heads):
            attend, _, _, value = attention_weights(
                joint, col_ref[seq], row_ref[seq], head, heads, size
            )
            mixed_ref[rows, head * size : (head + 1) * size] = dot(
                attend.astype(HALF), value
            ).astype(HALF)


def attention_back_kernel(heads, size, count, joint_ref, col_ref, row_ref, grad_ref, out_ref):
    length = joint_ref.shape[0] // count
    for seq in range(count):
        rows = slice(seq * length, (seq + 1) * length)
        joint = joint_ref[rows, :]
        for head in range(heads):
            attend, query, key, value = attention_weights(
                joint, col_ref[seq], row_ref[seq], head, heads, size
            )
            grad = grad_ref[rows, head * size : (head + 1) * size]
            attend_grad = contract_cols(grad, value)
            score_grad = (
                attend * (attend_grad - jnp.sum(attend_grad * attend, axis=-1, keepdims=True))
            ).astype(HALF)
            parts = (
                dot(score_grad, key) * size ** (-0.5),
                contract_rows(score_grad, query) * size ** (-0.5),
                contract_rows(attend.astype(HALF), grad),
            )
            for part, part_grad in enumerate(parts):
                start = (part * heads + head) * size
                out_ref[rows, start : start + size] = part_grad.astype(HALF)


def attention_call(kernel, joint, codes_col, codes_row, more, width, heads, size):
    seqs, length, _ = codes_col.shape
    count = 2 if seqs % 2 == 0 else 1
    wide = [joint] + more
    specs = [pl.BlockSpec((count * length, a.shape[1]), lambda i: (i, 0)) for a in wide]
    code_specs = [
        pl.BlockSpec((count, length, 2), lambda i: (i, 0, 0)),
        pl.BlockSpec((count, 2, length), lambda i: (i, 0, 0)),
    ]
    steps = 2 if kernel is attention_kernel else 6
    return pl.pallas_call(
        functools.partial(kernel, heads, size, count),
        grid=(seqs // count,),
        out_shape=jax.ShapeDtypeStruct((joint.shape[0], width), HALF),
        in_specs=specs[:1] + code_specs + specs[1:],
        out_specs=pl.BlockSpec((count * length, width), lambda i: (i, 0)),
        compiler_params=pltpu.CompilerParams(vmem_limit_bytes=16 * 2**20),
        cost_estimate=pl.CostEstimate(
            flops=2 * steps * seqs * heads * length * length * size,
            bytes_accessed=2 * joint.size * 2,
            transcendentals=seqs * heads * length * length,
        ),
    )(joint, codes_col, codes_row, *more)


GROUP_OFFSETS = [(ju, jc, jt) for ju in (0, 1) for jc in (0, 1) for jt in (0, 1)]


def member(index, offsets):
    return tuple(index[axis] ^ offset for axis, offset in zip(GROUP, offsets))


def swap_members(lay, blocks):
    return list(blocks[:1]) + [
        lay.swap_group(block, *offsets) for block, offsets in zip(blocks[1:], GROUP_OFFSETS[1:])
    ]


def gather_rows(lay, parts):
    pieces = [part.finish() for part in parts]
    rows, width = pieces[0][0, 0].shape
    sources = [(part, key) for part in range(len(parts)) for key in pieces[part]]

    def plan(index):
        return [
            (i, None, 0, (index["a"] ^ ja, index["b"] ^ jb, part))
            for i, (part, (ja, jb)) in enumerate(sources)
        ]

    shape = (lay.a, lay.b, len(parts), rows, width)
    full = move(plan, [shape], [pieces[part][key] for part, key in sources])[0]
    return full.reshape(-1, width)


def spread_slices(lay, shards, spans, start):
    rows = shards[0].shape[0]
    widths = [sum(size for _, size in span(0, 0, 0)) for span in spans]

    def pick(index):
        copies = []
        for i, offsets in enumerate(GROUP_OFFSETS):
            done = 0
            for number, span in enumerate(spans):
                for start, size in span(*member(index, offsets)):
                    copies.append(
                        (number, (slice(None), pl.ds(start, size)), i, (slice(None), pl.ds(done, size)))
                    )
                    done += size
        return copies

    def pile(index):
        copies = []
        for i in range(8):
            done = 0
            for number, width in enumerate(widths):
                copies.append((i, (slice(None), pl.ds(done, width)), number, (i,)))
                done += width
        return copies

    blocks = [after(block, start) for block in move(pick, [(rows, sum(widths))] * 8, shards)]
    received = swap_members(lay, blocks)
    return move(pile, [(8, rows, width) for width in widths], received)


def gather_slices(lay, copies):
    pieces = copies.finish()
    _, rows, width = pieces[0, 0].shape
    keys = list(pieces)

    def plan(index):
        moves = []
        for i, (ja, jb) in enumerate(keys):
            for slot, offsets in enumerate(GROUP_OFFSETS):
                u, c, t = member(index, offsets)
                moves.append((i, (slot,), 0, (u, c, index["a"] ^ ja, t, index["b"] ^ jb)))
        return moves

    shape = (lay.u, 2, lay.a, 2, lay.b, rows, width)
    return move(plan, [shape], [pieces[key] for key in keys])[0].reshape(-1, width)


def reduce_rows(lay, gradient):
    me_a, me_b = lax.axis_index("a"), lax.axis_index("b")
    shaped = gradient.reshape(lay.a, lay.b, -1, gradient.shape[1])
    return Reduction(
        lay,
        {
            (ja, jb): lax.dynamic_slice(
                shaped, (me_a ^ ja, me_b ^ jb, 0, 0), (1, 1) + shaped.shape[2:]
            )[0, 0]
            for ja in range(lay.a)
            for jb in range(lay.b)
        },
    )


def reduce_slices(lay, gradient):
    me_a, me_b = lax.axis_index("a"), lax.axis_index("b")
    width = gradient.shape[1]
    shaped = gradient.reshape(lay.u * 2, lay.a, 2, lay.b, -1, width)
    size = (lay.u * 2, 1, 2, 1, shaped.shape[4], width)
    return Reduction(
        lay,
        {
            (ja, jb): lax.dynamic_slice(shaped, (0, me_a ^ ja, 0, me_b ^ jb, 0, 0), size)[:, 0, :, 0]
            for ja in range(lay.a)
            for jb in range(lay.b)
        },
    )


def member_blocks(lay, summed):
    shaped = summed.reshape((lay.u, 2, 2) + summed.shape[2:])
    me = {axis: lax.axis_index(axis) for axis in GROUP}
    return [
        lax.dynamic_slice(shaped, member(me, offsets) + (0, 0), (1, 1, 1) + shaped.shape[3:])[0, 0, 0]
        for offsets in GROUP_OFFSETS
    ]


def join_slices(lay, blocks, spans, columns):
    rows = blocks[0].shape[0]

    def plan(index):
        copies = []
        for i, offsets in enumerate(GROUP_OFFSETS):
            done = 0
            for start, size in spans(*member(index, offsets)):
                copies.append(
                    (i, (slice(None), pl.ds(done, size)), 0, (slice(None), pl.ds(start, size)))
                )
                done += size
        return copies

    return move(plan, [(rows, columns)], blocks)[0]


def gather_all(lay, block):
    early = None
    for axis in ("t", "a", "u", "c", "b"):
        parts = [block]
        for bit in lay.bits(axis):
            parts = parts + [lay.swap(part, axis, bit) for part in parts]
        block = jnp.stack(parts)
        early = block if axis == "a" else early
    return block.transpose(3, 0, 2, 1, 4, 5, 6), early


def sum_all(lay, value):
    for axis in ("c", "u", "t", "b", "a"):
        for bit in lay.bits(axis):
            value = value + lay.swap(value, axis, bit)
    return value


def dot(left, right):
    return jnp.dot(left, right, preferred_element_type=FULL)


def contract_rows(left, right):
    return lax.dot_general(left, right, (((0,), (0,)), ((), ())), preferred_element_type=FULL)


def contract_cols(left, right):
    return lax.dot_general(left, right, (((1,), (1,)), ((), ())), preferred_element_type=FULL)


def rms_scale(values, gain_row):
    return (
        values
        * lax.rsqrt(jnp.mean(values * values, axis=-1, keepdims=True) + NORM_EPSILON)
        * gain_row
    )


def rms_back(values, gain_row, gradient):
    inverse = lax.rsqrt(jnp.mean(values * values, axis=-1, keepdims=True) + NORM_EPSILON)
    scaled = gradient * gain_row
    along = jnp.mean(values * scaled, axis=-1, keepdims=True)
    value_grad = inverse * scaled - values * (inverse * inverse * inverse * along)
    return value_grad, jnp.sum(gradient * values * inverse, axis=0)


def target_masks(token_ids, clip_ids, frame_ids, context_frames, valid_mask):
    next_ids = jnp.concatenate([token_ids[:, 1:], jnp.zeros_like(token_ids[:, :1])], axis=1)
    never = jnp.zeros_like(clip_ids[:, :1]) > 0
    same_clip = jnp.concatenate([clip_ids[:, 1:] == clip_ids[:, :-1], never], axis=1)
    after_context = jnp.concatenate([frame_ids[:, 1:] > context_frames[:, None], never], axis=1)
    counted = ((valid_mask > 0) & same_clip & after_context).astype(FULL)
    return (next_ids, counted, valid_mask.astype(FULL))


def adam_update(master, moment, variance, gradient, rate, decay):
    new_mean = BETA_FIRST * moment + (1.0 - BETA_FIRST) * gradient
    new_square = BETA_SECOND * variance + (1.0 - BETA_SECOND) * gradient * gradient
    mean_hat = new_mean / (1.0 - BETA_FIRST**STEP)
    square_hat = new_square / (1.0 - BETA_SECOND**STEP)
    new_master = master - rate * (mean_hat / (jnp.sqrt(square_hat) + ADAM_EPSILON) + decay * master)
    return (new_master, new_mean, new_square)


def local(lay, *arguments):
    token_ids, clip_ids, frame_ids, context_frames, valid_mask = arguments[:5]
    masters, moments, variances = arguments[5::3], arguments[6::3], arguments[7::3]
    lookup_half, mixing_half, merging_half, widening_half, narrowing_half, readout_half = (
        master.astype(HALF) for master in masters[:6]
    )
    seqs, length = token_ids.shape
    model_width = lookup_half.shape[1]
    head_size = model_width // HEADS
    me = {axis: lax.axis_index(axis) for axis in ALL}
    me_flat = (((me["u"] * 2 + me["c"]) * lay.a + me["a"]) * 2 + me["t"]) * lay.b + me["b"]

    gain_cols = masters[6].shape[1]
    packed = jnp.concatenate(
        [
            token_ids.astype(FULL).reshape(-1),
            clip_ids.astype(FULL).reshape(-1),
            frame_ids.astype(FULL).reshape(-1),
            valid_mask.astype(FULL).reshape(-1),
            context_frames.astype(FULL),
            lax.reduce_precision(masters[6], 8, 7).reshape(-1),
        ]
    )
    pack_size = packed.shape[0]
    packed = jnp.pad(packed, (0, -pack_size % 1024)).reshape(8, -1)
    everyone, early = gather_all(lay, packed)
    everyone = everyone.reshape(lay.a, lay.b, lay.u, 2, 2, -1)[..., :pack_size]
    flat_all = everyone.reshape(lay.devices, pack_size)
    span = seqs * length

    def unpack(rows):
        ids = [
            rows[:, i * span : (i + 1) * span].reshape(-1, length).astype(jnp.int32) for i in range(4)
        ]
        context = rows[:, 4 * span : 4 * span + seqs].reshape(-1).astype(jnp.int32)
        return ids[0], ids[1], ids[2], context, ids[3]

    _, counted_all, valid_all = target_masks(*unpack(flat_all))
    mask_count, valid_count = jnp.sum(counted_all), jnp.sum(valid_all)
    gains_mine = flat_all[:, 4 * span + seqs :].reshape(lay.devices, 3, gain_cols)
    place_of = jnp.arange(lay.devices)
    rel = place_of ^ me_flat
    rel_t = (rel // lay.b) % 2
    rel_b = rel % lay.b
    rel_a = (rel // (2 * lay.b)) % lay.a
    rel_uc = rel // (2 * lay.a * lay.b)
    spot = ((rel_a * lay.b + rel_b) * lay.u * 2 + rel_uc) * 2 + rel_t
    gain_rows = gains_mine[spot].transpose(1, 0, 2).reshape(3, model_width)

    by_core = everyone[0, 0].transpose(1, 0, 2, 3)
    turned = by_core.transpose(0, 2, 1, 3)
    first_core = me["c"] == 0
    group_rows = jnp.concatenate(
        [
            jnp.where(first_core, turned[0], by_core[0]).reshape(4, pack_size),
            jnp.where(first_core, by_core[1], turned[1]).reshape(4, pack_size),
        ]
    )
    token_g, clip_g, frame_g, context_g, valid_g = unpack(group_rows)
    next_g, counted_g, valid_g = target_masks(token_g, clip_g, frame_g, context_g, valid_g)
    group_seqs = token_g.shape[0]
    flat_tokens, flat_next = token_g.reshape(-1), next_g.reshape(-1)
    counted_flat, valid_flat = counted_g.reshape(-1), valid_g.reshape(-1)
    tokens = flat_tokens.shape[0]

    hidden = narrowing_half.shape[0]
    code_count = readout_half.shape[1] // 8

    def mixing_spans(u, c, t):
        return [
            (part * model_width + (((u * 2 + c) * lay.a + a) * 2 + t) * head_size, head_size)
            for part in range(3)
            for a in range(lay.a)
        ]

    def widening_spans(u, c, t):
        size = lay.b * hidden
        return [((((u * 2 + c) * lay.a + a) * 2 + t) * size, size) for a in range(lay.a)]

    def readout_spans(u, c, t):
        return [(((u * 2 + c) * 2 + t) * code_count, code_count)]

    half_rows = lookup_half.shape[0] // 2
    table_top = Copies(lay, lookup_half[:half_rows], early)
    (mixing_spread,) = spread_slices(lay, [mixing_half], [mixing_spans], early)
    table_low = Copies(lay, lookup_half[half_rows:], [table_top.over_a, mixing_spread])
    widening_spread, readout_spread = spread_slices(
        lay, [widening_half, readout_half], [widening_spans, readout_spans], mixing_spread
    )
    mixing_copies = Copies(lay, mixing_spread, table_low.over_a)
    table = gather_rows(lay, [table_top, table_low])

    table_rows = lookup_half.shape[0]
    row_ids = (
        (((me["u"] * 2 + me["c"]) * lay.a + jnp.arange(lay.a)[:, None, None]) * 2 + me["t"]) * lay.b
        + jnp.arange(lay.b)[None, :, None]
    ) * table_rows + jnp.arange(table_rows)[None, None, :]
    chosen = (flat_tokens[:, None] == row_ids.reshape(1, -1)).astype(HALF)
    chosen_then = after(chosen, [widening_spread, readout_spread])
    embedded = scatter_group(
        lay,
        chosen_then,
        lambda rows: dot(rows, table),
        WIRE_HALF,
        None,
        mixing_copies.over_a,
    )
    merging_copies = Copies(lay, merging_half, mixing_copies.over_a)

    normed_one = gather_group(
        lay, rms_scale(embedded, gain_rows[0]).astype(HALF), merging_copies.over_a
    )
    widening_copies = Copies(lay, widening_spread, merging_copies.over_a)
    mixing = gather_slices(lay, mixing_copies)
    merging = gather_rows(lay, [merging_copies])
    joint = dot(normed_one, mixing).astype(HALF)
    codes = jnp.stack([clip_g, frame_g], axis=1)
    codes_col = codes.transpose(0, 2, 1)
    mixed_heads = attention_call(
        attention_kernel, joint, codes_col, codes, [], merging.shape[0], lay.a, head_size
    )
    narrowing_copies = Copies(lay, narrowing_half, widening_copies.over_a)
    stream_one = embedded + scatter_group(
        lay,
        mixed_heads,
        lambda rows: dot(rows, merging),
        WIRE_FORWARD,
        widening_copies.over_a,
    )

    normed_two = gather_group(
        lay, rms_scale(stream_one, gain_rows[1]).astype(HALF), narrowing_copies.over_a
    )
    readout_copies = Copies(lay, readout_spread, narrowing_copies.over_a)
    widening = gather_slices(lay, widening_copies)
    narrowing = gather_rows(lay, [narrowing_copies])
    widened = dot(normed_two, widening)
    activated = jax.nn.gelu(widened).astype(HALF)
    stream_two = stream_one + scatter_group(
        lay, activated,
        lambda rows: dot(rows, narrowing), WIRE_FORWARD
    )

    normed_three = gather_group(
        lay, rms_scale(stream_two, gain_rows[2]).astype(HALF), readout_copies.over_a
    )
    readout = gather_slices(lay, readout_copies)
    logits = dot(normed_three, readout)
    code_start = ((me["u"] * 2 + me["c"]) * 2 + me["t"]) * code_count
    hit = (code_start + lax.broadcasted_iota(jnp.int32, logits.shape, 1)) == flat_next[:, None]
    top = jnp.max(logits, axis=-1)
    total = jnp.sum(jnp.exp(logits - top[:, None]), axis=-1)
    picked = jnp.sum(jnp.where(hit, logits, 0.0), axis=-1)
    state = jnp.stack([top, total, picked]).reshape(3, 2, 2, 2, -1)
    for stage in range(3):
        if stage == 0:
            other = jnp.flip(lay.swap(state, "c"), axis=1)
        else:
            other = (lay.swap_first, lay.swap_second)[stage - 1](state)
            other = jnp.stack(
                [jnp.flip(other[:, 0], axis=3 - stage), jnp.flip(other[:, 1], axis=stage)], axis=1
            )
        joined = jnp.maximum(state[0], other[0])
        state = jnp.stack(
            [
                joined,
                state[1] * jnp.exp(state[0] - joined) + other[1] * jnp.exp(other[0] - joined),
                state[2] + other[2],
            ]
        )
    top, total, picked = state.reshape(3, tokens)
    log_total = top + jnp.log(total)
    mine = seqs * length
    cross_part = jnp.sum(((log_total - picked) * counted_flat)[:mine])
    square_part = jnp.sum((log_total * log_total * valid_flat)[:mine])
    total_grad = (
        counted_flat / mask_count + 2.0 * SQUARE_COEF * log_total * valid_flat / valid_count
    )
    logit_grad = (
        jnp.exp(logits - log_total[:, None]) * total_grad[:, None]
        - jnp.where(hit, (counted_flat / mask_count)[:, None], 0.0)
    ).astype(HALF)

    readout_red = reduce_slices(lay, contract_rows(normed_three, logit_grad))
    sent = readout_red.prepare()
    normed_three_grad = scatter_group(
        lay,
        logit_grad,
        lambda rows: contract_cols(rows, readout),
        WIRE_BACK,
        sent,
    )
    readout_red.step()
    stream_two_grad, gain_three_grad = rms_back(stream_two, gain_rows[2], normed_three_grad)

    sent = readout_red.prepare()
    branch_grad = gather_group(lay, stream_two_grad.astype(HALF), None, sent)
    _, gelu_pull = jax.vjp(jax.nn.gelu, widened)
    widened_grad = gelu_pull(contract_cols(branch_grad, narrowing))[0].astype(HALF)
    narrowing_red = reduce_rows(lay, contract_rows(activated, branch_grad))
    widening_red = reduce_slices(lay, contract_rows(normed_two, widened_grad))
    sent = narrowing_red.prepare() + widening_red.prepare()
    readout_came = readout_red.step(None, sent)
    normed_two_grad = scatter_group(
        lay,
        widened_grad,
        lambda rows: contract_cols(rows, widening),
        WIRE_BACK,
        sent,
        readout_came,
    )
    narrowing_red.step()
    widening_red.step()
    stream_one_part, gain_two_grad = rms_back(stream_one, gain_rows[1], normed_two_grad)
    stream_one_grad = stream_two_grad + stream_one_part

    sent = narrowing_red.prepare()
    output_grad = gather_group(lay, stream_one_grad.astype(HALF), None, sent)
    narrowing_came = narrowing_red.step()
    heads_grad = contract_cols(output_grad, merging).astype(HALF)
    joint_grad = attention_call(
        attention_back_kernel, joint, codes_col, codes, [heads_grad], joint.shape[1], lay.a, head_size
    )
    mixing_red = reduce_slices(lay, contract_rows(normed_one, joint_grad))
    merging_red = reduce_rows(lay, contract_rows(mixed_heads, output_grad))
    sent = mixing_red.prepare() + merging_red.prepare()
    late = widening_red.prepare()
    normed_one_grad = scatter_group(
        lay,
        joint_grad,
        lambda rows: contract_cols(rows, mixing),
        WIRE_BACK,
        sent,
        late,
    )
    widening_came = widening_red.step()
    mixing_red.step()
    merging_red.step()
    embedded_part, gain_one_grad = rms_back(embedded, gain_rows[0], normed_one_grad)
    embedded_grad = stream_one_grad + embedded_part

    sent = mixing_red.prepare() + merging_red.prepare()
    embedded_all = gather_group(
        lay, embedded_grad.astype(HALF), None, [sent, narrowing_came]
    )
    mixing_came = mixing_red.step()
    merging_came = merging_red.step()
    readout_blocks = [
        after(part, embedded_all)
        for part in member_blocks(lay, readout_red.finish().astype(SLICE_WIRE))
    ]
    readout_blocks = swap_members(lay, readout_blocks)
    lookup_reds = []
    for part in range(2):
        picked_rows = chosen.reshape(tokens, -1, 2, half_rows)[:, :, part].reshape(tokens, -1)
        lookup_reds.append(reduce_rows(lay, contract_rows(picked_rows, embedded_all)))
    sent = [lookup_red.prepare() for lookup_red in lookup_reds]
    came = [lookup_red.step() for lookup_red in lookup_reds]
    widening_blocks = [
        after(part, sent)
        for part in member_blocks(lay, widening_red.finish().astype(SLICE_WIRE))
    ]
    widening_blocks = swap_members(lay, widening_blocks)
    mixing_blocks = member_blocks(lay, mixing_red.finish().astype(SLICE_WIRE))
    mixing_blocks = swap_members(lay, mixing_blocks)
    lookup_reds[0].prepare()
    lookup_reds[0].step(None, [widening_blocks, readout_blocks])
    lookup_reds[1].prepare()
    lookup_reds[1].step(None, mixing_blocks)
    gain_grads = jnp.stack([gain_one_grad, gain_two_grad, gain_three_grad])
    gain_grads = sum_all(lay, after(gain_grads, sent))
    scaling_sum = lax.dynamic_slice(gain_grads, (0, me_flat * gain_cols), (3, gain_cols))
    lookup_sum = jnp.concatenate([lookup_red.finish() for lookup_red in lookup_reds])
    narrowing_sum, merging_sum = narrowing_red.finish(), merging_red.finish()
    readout_sum = join_slices(lay, readout_blocks, readout_spans, readout_half.shape[1])
    widening_sum = join_slices(lay, widening_blocks, widening_spans, widening_half.shape[1])
    mixing_sum = join_slices(lay, mixing_blocks, mixing_spans, mixing_half.shape[1])

    gradients = [
        to_full(gradient)
        for gradient in (
            lookup_sum,
            mixing_sum,
            merging_sum,
            widening_sum,
            narrowing_sum,
            readout_sum,
            scaling_sum,
        )
    ]
    local_square = sum((jnp.sum(gradient * gradient) for gradient in gradients))
    sums = sum_all(lay, jnp.stack([cross_part, square_part, local_square]))
    norm_value = jnp.sqrt(sums[2])
    clip_factor = jnp.minimum(1.0, CLIP_NORM / norm_value)
    outputs = [jnp.stack([sums[0], mask_count, sums[1], valid_count]), norm_value]
    for index in range(7):
        updated = adam_update(
            masters[index],
            moments[index],
            variances[index],
            gradients[index] * clip_factor,
            LEARN_RATES[index],
            DECAY_RATES[index],
        )
        outputs.extend(updated)
        if index < 6:
            outputs.append(updated[0].astype(HALF))
    return tuple(outputs)


def solution(mesh):
    lay = Layout(mesh)
    row, matrix, columns = P(ALL), P(ALL, None), P(None, ALL)
    in_specs = (matrix, matrix, matrix, row, matrix) + (matrix,) * 18 + (columns,) * 3
    out_specs = (P(), P()) + (matrix,) * 24 + (columns,) * 3
    return jax.shard_map(
        functools.partial(local, lay),
        mesh=lay.mesh,
        in_specs=in_specs,
        out_specs=out_specs,
        check_vma=False,
    )
```
